256 devices in a mesh: context: 32 (over x, y, core), tensor: 8 (over z).
Axes of the slice: x: 4, y: 4, z: 8, core: 2. Of those that a mesh axis runs over, the one named last changes fastest.
Arguments:
- inner_in: bfloat16 [4096, 8192], P('context', 'tensor'), may hold values from -6 to 6
- gate_in: bfloat16 [4096, 8192], P('context', 'tensor'), may hold values from -6 to 6
- out_grad: bfloat16 [4096, 8192], P('context', 'tensor'), may hold values from -6 to 6
- kernel: float32 [8192, 4], P('tensor'), may hold values from -3 to 3
- kernel_shift: float32 [8192], P('tensor'), may hold values from -0.5 to 0.5
- select_proj: bfloat16 [544, 8192], P(None, 'tensor'), may hold values from -0.0625 to 0.0625
- delta_proj: bfloat16 [8192, 512], P('tensor'), may hold values from -0.25 to 0.25
- delta_bias: float32 [8192], P('tensor'), may hold values from -7 to -2
- decay_log: float32 [8192, 16], P('tensor'), may hold values from -1 to 2.8
- skip_gain: float32 [8192], P('tensor'), may hold values from 0.5 to 1.5
Outputs:
- inner_grad: bfloat16 [4096, 8192], P('context', 'tensor')
- gate_grad: bfloat16 [4096, 8192], P('context', 'tensor')
- kernel_grad: float32 [8192, 4], P('tensor')
- shift_grad: float32 [8192], P('tensor')
- select_grad: float32 [544, 8192], P('context', 'tensor')
- delta_grad: float32 [8192, 512], P('tensor', 'context')
- bias_grad: float32 [8192], P('tensor')
- decay_grad: float32 [8192, 16], P('tensor')
- skip_grad: float32 [8192], P('tensor')
The draws below stay inside these ranges and needn't reach their ends.
All inputs are finite; a program needn't handle non-finite values.
Results may differ from the reference program's by a relative error of at most 0.017.
Values may be sent and summed in bfloat16 or wider, within the bound.
A program may use at most 128 MiB of HBM per device.

```python
import jax
import jax.numpy as jnp
from jax import lax

DI = 8192
N_STATE = 16
RANK = 512
KCONV = 4
PROJ = 544
TOKENS = 4096


def shard_levels(rng, shape, cuts, low, top_value):
    level = 1.0
    for axis_at, shards_of in cuts:
        heights = jax.random.uniform(jax.random.fold_in(jax.random.fold_in(rng, 6), axis_at), (shards_of,), jnp.float32, low / len(cuts), top_value / len(cuts))
        level = level * jnp.repeat(jnp.exp(heights), shape[axis_at] // shards_of).reshape((-1,) + (1,) * (len(shape) - 1 - axis_at))
    return level


def centred(rng, dims, width, most, cuts=(), kind=jnp.bfloat16):
    values = jax.random.normal(rng, dims, jnp.float32) * width
    if len(cuts) > 0:
        values = shard_levels(rng, dims, cuts, -0.22, 0.18) * values
    return jnp.clip(values, min=-most, max=most).astype(kind)


def setup_inputs(seed: int = 0) -> dict:
    key_of = jax.random.split(jax.random.key(seed), 11)
    return {
        "inner_in": centred(key_of[0], (TOKENS, DI), 1.0, 6.0, ((0, 32), (1, 8))),
        "gate_in": centred(key_of[1], (TOKENS, DI), 1.0, 6.0, ((0, 32), (1, 8))),
        "out_grad": centred(key_of[2], (TOKENS, DI), 1.0, 6.0, ((0, 32), (1, 8))),
        "kernel": centred(key_of[3], (DI, KCONV), KCONV ** -0.5, 3.0, ((0, 8),), jnp.float32),
        "kernel_shift": jnp.clip(jax.random.uniform(key_of[4], (DI,), jnp.float32, -0.5, 0.5) * shard_levels(key_of[4], (DI,), ((0, 8),), -0.4, 0.0), -0.5, 0.5),
        "select_proj": centred(key_of[5], (PROJ, DI), DI ** -0.5, 0.0625, ((1, 8),)),
        "delta_proj": centred(key_of[6], (DI, RANK), RANK ** -0.5, 0.25, ((0, 8),)),
        "delta_bias": jnp.clip(-7.0 + 5.0 * jax.random.uniform(key_of[7], (DI,), jnp.float32) ** shard_levels(key_of[7], (DI,), ((0, 8),), -0.2, 0.2), -7.0, -2.0),
        "decay_log": jnp.clip(-1.0 + 3.8 * jax.random.uniform(key_of[8], (DI, N_STATE), jnp.float32) ** shard_levels(key_of[8], (DI, N_STATE), ((0, 8),), -0.2, 0.2), -1.0, 2.8),
        "skip_gain": jnp.clip(0.5 + 1.0 * jax.random.uniform(key_of[9], (DI,), jnp.float32) ** shard_levels(key_of[9], (DI,), ((0, 8),), -0.2, 0.2), 0.5, 1.5),
    }


def silu_slope(values):
    logistic = jax.nn.sigmoid(values)
    return logistic * (1.0 + values * (1.0 - logistic))


def reference(inner_in, gate_in, out_grad, kernel, kernel_shift, select_proj, delta_proj, delta_bias, decay_log, skip_gain):
    tokens = inner_in.shape[0]
    padded = jnp.concatenate([jnp.zeros((KCONV - 1, DI), jnp.float32), inner_in.astype(jnp.float32)], 0)
    conv_pre = jnp.zeros((tokens, DI), jnp.float32) + kernel_shift[None, :]
    for position in range(KCONV):
        conv_pre = conv_pre + kernel[:, position][None, :] * padded[position:position + tokens]
    conv_out = jax.nn.silu(conv_pre)
    conv_half = conv_out.astype(jnp.bfloat16)
    projected = jnp.dot(conv_half, select_proj.T, preferred_element_type=jnp.float32)
    low_rank = projected[:, :RANK].astype(jnp.bfloat16)
    input_mat = projected[:, RANK:RANK + N_STATE]
    output_mat = projected[:, RANK + N_STATE:]
    delta_raw = jnp.dot(low_rank, delta_proj.T, preferred_element_type=jnp.float32) + delta_bias[None, :]
    deltas = jax.nn.softplus(delta_raw)
    decay_rate = -jnp.exp(decay_log).T
    gate_value = gate_in.astype(jnp.float32)
    out_cot = out_grad.astype(jnp.float32) * jax.nn.silu(gate_value)
    breadth = min(256, DI)
    groups = DI // breadth

    def channel_block(pieces):
        conv_part, delta_part, cot_part, rate_part, skip_part = pieces
        decays = jnp.exp(delta_part[:, None, :] * rate_part[None])
        inflow = (delta_part * conv_part)[:, None, :] * input_mat[:, :, None]

        def forward(carried, element):
            carried = element[0] * carried + element[1]
            return carried, carried

        zero_state = jnp.zeros((N_STATE, breadth), jnp.float32)
        _, states = lax.scan(forward, zero_state, (decays, inflow))
        source = output_mat[:, :, None] * cot_part[:, None, :]
        follow = jnp.concatenate([decays[1:], jnp.ones((1, N_STATE, breadth), jnp.float32)], 0)
        _, adjoint = lax.scan(forward, zero_state, (follow, source), reverse=True)
        earlier = jnp.concatenate([zero_state[None], states[:-1]], 0)
        outputs = jnp.einsum('tnc,tn->tc', states, output_mat) + skip_part[None, :] * conv_part
        along_input = jnp.einsum('tnc,tn->tc', adjoint, input_mat)
        direct = skip_part[None, :] * cot_part + delta_part * along_input
        weighted = adjoint * decays * earlier
        delta_cot = jnp.sum(weighted * rate_part[None], axis=1) + conv_part * along_input
        input_cot = jnp.einsum('tnc,tc->tn', adjoint, delta_part * conv_part)
        output_cot = jnp.einsum('tnc,tc->tn', states, cot_part)
        rate_cot = jnp.sum(weighted * delta_part[:, None, :], axis=0)
        return outputs, direct, delta_cot, input_cot, output_cot, rate_cot

    def blocks(array):
        return array.reshape(tokens, groups, breadth).transpose(1, 0, 2)

    def unblock(array):
        return array.transpose(1, 0, 2).reshape(tokens, DI)

    rates = decay_rate.reshape(N_STATE, groups, breadth).transpose(1, 0, 2)
    results = lax.map(channel_block, (blocks(conv_out), blocks(deltas), blocks(out_cot), rates, skip_gain.reshape(groups, breadth)))
    outputs = unblock(results[0])
    direct = unblock(results[1])
    delta_cot = unblock(results[2])
    input_cot = jnp.sum(results[3], 0)
    output_cot = jnp.sum(results[4], 0)
    rate_total = results[5].transpose(1, 0, 2).reshape(N_STATE, DI)
    gate_grad = (out_grad.astype(jnp.float32) * outputs * silu_slope(gate_value)).astype(jnp.bfloat16)
    raw_cot = delta_cot * jax.nn.sigmoid(delta_raw)
    raw_half = raw_cot.astype(jnp.bfloat16)
    rank_cot = jnp.dot(raw_half, delta_proj, preferred_element_type=jnp.float32)
    delta_grad = jnp.dot(raw_half.T, low_rank, preferred_element_type=jnp.float32)
    select_cot = jnp.concatenate([rank_cot, input_cot, output_cot], 1).astype(jnp.bfloat16)
    select_grad = jnp.dot(select_cot.T, conv_half, preferred_element_type=jnp.float32)
    conv_cot = direct + jnp.dot(select_cot, select_proj, preferred_element_type=jnp.float32)
    pre_cot = conv_cot * silu_slope(conv_pre)
    shift_grad = jnp.sum(pre_cot, 0)
    kernel_grad = jnp.stack([jnp.sum(pre_cot * padded[position:position + tokens], 0) for position in range(KCONV)], 1)
    trailing = jnp.concatenate([pre_cot, jnp.zeros((KCONV - 1, DI), jnp.float32)], 0)
    inner_grad = jnp.zeros((tokens, DI), jnp.float32)
    for position in range(KCONV):
        first_row = KCONV - 1 - position
        inner_grad = inner_grad + kernel[:, position][None, :] * trailing[first_row:first_row + tokens]
    inner_grad = inner_grad.astype(jnp.bfloat16)
    bias_grad = jnp.sum(raw_cot, 0)
    decay_grad = (rate_total * decay_rate).T
    skip_grad = jnp.sum(out_cot * conv_out, 0)
    return inner_grad, gate_grad, kernel_grad, shift_grad, select_grad, delta_grad, bias_grad, decay_grad, skip_grad
```

```python
import functools

import jax
import jax.numpy as jnp
from jax import lax
from jax.experimental import pallas as pl
from jax.experimental.pallas import tpu as pltpu
from jax.sharding import PartitionSpec as P

N = 16
RANK = 512
TAPS = 4
PROJ = 544
WIDE = 640
T = 128
C = 1024
H = 512
CTX = 32
TEN = 8
ROWS = T // TEN
LOG2E = 1.4426950408889634
MESH = pl.DeviceIdType.MESH
F32 = jnp.float32
BF16 = jnp.bfloat16
VMEM = pl.BlockSpec(memory_space=pltpu.VMEM)


def dot_nn(a, b):
    return lax.dot_general(a, b, (((1,), (0,)), ((), ())), preferred_element_type=F32)


def dot_nt(a, b):
    return lax.dot_general(a, b, (((1,), (1,)), ((), ())), preferred_element_type=F32)


def dot_tn(a, b):
    return lax.dot_general(a, b, (((0,), (0,)), ((), ())), preferred_element_type=F32)


def iota(shape, axis):
    return lax.broadcasted_iota(jnp.int32, shape, axis)


def sigmoid(v):
    return jax.nn.sigmoid(v)


def silu_slope(v):
    s = sigmoid(v)
    return s * (1.0 + v * (1.0 - s))


def split_tile(v):
    high = v.astype(BF16).astype(F32)
    return jnp.where(iota(v.shape, 1) < 64, high, v - high).astype(BF16)


class Exchange:
    def __init__(self, src, dst, send, recv, axis, size, same=False):
        self.src, self.dst, self.send, self.recv = src, dst, send, recv
        self.axis, self.size, self.same = axis, size, same

    def copy(self, off):
        me = lax.axis_index(self.axis)
        peer = lax.rem(me + off, self.size)
        return pltpu.make_async_remote_copy(
            src_ref=self.src.at[me] if self.same else self.src.at[peer],
            dst_ref=self.dst.at[me],
            send_sem=self.send.at[off],
            recv_sem=self.recv.at[off],
            device_id={self.axis: peer},
            device_id_type=MESH,
        )

    def start(self):
        lax.fori_loop(1, self.size, lambda off, _: (self.copy(off).start(), 0)[1], 0)

    def wait_recv(self):
        lax.fori_loop(1, self.size, lambda off, _: (self.copy(off).wait_recv(), 0)[1], 0)

    def wait_send(self):
        lax.fori_loop(1, self.size, lambda off, _: (self.copy(off).wait_send(), 0)[1], 0)


def greet(axis, size):
    me = lax.axis_index(axis)
    barrier = pltpu.get_barrier_semaphore()

    def signal(off, _):
        pl.semaphore_signal(
            barrier, inc=1, device_id={axis: lax.rem(me + off, size)}, device_id_type=MESH
        )
        return 0

    lax.fori_loop(1, size, signal, 0)


def to_neighbour(src, dst, send, recv, step):
    peer = lax.rem(lax.axis_index("context") + step + CTX, CTX)
    return pltpu.make_async_remote_copy(
        src_ref=src, dst_ref=dst, send_sem=send, recv_sem=recv,
        device_id={"context": peer}, device_id_type=MESH,
    )


def front_kernel(
    inner, taps, shift, wsel, pad, pre, proj,
    halo, wtail, part, got, hs, hr, ss, sr, gs, gr,
):
    ctx, ten = lax.axis_index("context"), lax.axis_index("tensor")
    barrier = pltpu.get_barrier_semaphore()
    for step in (1, CTX - 1):
        pl.semaphore_signal(
            barrier, inc=1, device_id={"context": lax.rem(ctx + step, CTX)}, device_id_type=MESH
        )
    greet("tensor", TEN)
    pl.semaphore_wait(barrier, TEN + 1)

    edge = to_neighbour(inner.at[pl.ds(T - 16, 16)], halo, hs, hr, 1)
    edge.start()
    tail = wsel[RANK:PROJ, :]
    wtail[0:32, :] = tail
    wtail[32:64, :] = jnp.zeros((32, C), BF16)
    wtail[64:96, :] = tail
    wtail[96:128, :] = jnp.zeros((32, C), BF16)
    pad[16:, :] = inner[...].astype(F32)
    edge.wait()
    pad[0:16, :] = halo[...].astype(F32) * (ctx > 0).astype(F32)

    value = jnp.zeros((T, C), F32) + shift[...]
    for k in range(TAPS):
        value = value + taps[k : k + 1, :] * pad[pl.ds(16 - TAPS + 1 + k, T), :]
    pre[...] = value
    half = (value * sigmoid(value)).astype(BF16)
    part[:, :, :RANK] = dot_nt(half, wsel[:RANK, :]).astype(BF16).reshape(TEN, ROWS, RANK)
    part[:, :, RANK:] = split_tile(dot_nt(half, wtail[...])).reshape(TEN, ROWS, 128)

    scatter = Exchange(part, got, ss, sr, "tensor", TEN)
    scatter.start()
    got[ten] = part[ten]
    scatter.wait_recv()
    total = jnp.sum(got[...].astype(F32), axis=0)
    bc = total[:, RANK:]
    bc = bc + pltpu.roll(bc, 64, 1)
    proj[ten, :, :RANK] = total[:, :RANK].astype(BF16)
    proj[ten, :, RANK:] = split_tile(bc)
    gather = Exchange(proj, proj, gs, gr, "tensor", TEN, same=True)
    gather.start()
    gather.wait_recv()
    scatter.wait_send()
    gather.wait_send()


def front(inner, taps, shift, wsel):
    return pl.pallas_call(
        front_kernel,
        out_shape=(
            jax.ShapeDtypeStruct((T + 16, C), F32),
            jax.ShapeDtypeStruct((T, C), F32),
            jax.ShapeDtypeStruct((TEN, ROWS, WIDE), BF16),
        ),
        in_specs=[VMEM] * 4,
        out_specs=(VMEM,) * 3,
        scratch_shapes=[
            pltpu.VMEM((16, C), BF16),
            pltpu.VMEM((128, C), BF16),
            pltpu.VMEM((TEN, ROWS, WIDE), BF16),
            pltpu.VMEM((TEN, ROWS, WIDE), BF16),
            pltpu.SemaphoreType.DMA,
            pltpu.SemaphoreType.DMA,
        ] + [pltpu.SemaphoreType.DMA((TEN,))] * 4,
        compiler_params=pltpu.CompilerParams(
            collective_id=0, has_side_effects=True, vmem_limit_bytes=32 << 20
        ),
        name="front",
    )(inner, taps, shift, wsel)


def spread(tile, first):
    rows = T * N
    repeat = (iota((rows, T), 0) // N == iota((rows, T), 1)).astype(BF16)
    each = dot_nn(repeat, tile)
    mine = iota((rows, 128), 1) % 64 == iota((rows, 128), 0) % N + first
    return dot_nn(jnp.where(mine, each, 0.0).astype(BF16), jnp.ones((128, 128), BF16))


def summary_kernel(
    pre, proj, wdelta, bias, dlog, gate, grad, raw, deltas, dx, ocot, bspread, cspread, ends
):
    flat = proj[...].reshape(T, WIDE)
    value = dot_nt(flat[:, :RANK], wdelta[...]) + bias[...]
    raw[...] = value
    step = jnp.maximum(value, 0.0) + jnp.log1p(jnp.exp(-jnp.abs(value)))
    deltas[...] = step
    v = pre[...]
    dx[...] = step * (v * sigmoid(v))
    g = gate[...].astype(F32)
    ocot[...] = grad[...].astype(F32) * (g * sigmoid(g))
    bspread[...] = spread(flat[:, RANK:], 0).reshape(T, N, 128)
    cspread[...] = spread(flat[:, RANK:], N).reshape(T, N, 128)

    def half(h, _):
        lanes = pl.ds(pl.multiple_of(h * H, H), H)
        rate = jnp.exp(dlog[:, lanes]) * (-LOG2E)

        def steps(block, carried):
            state, decay, flow = carried
            for i in range(8):
                t = block * 8 + i
                row = pl.ds(t, 1)
                d = jnp.exp2(deltas[row, lanes] * rate)
                b = jnp.concatenate([bspread[t]] * (H // 128), 1)
                c = jnp.concatenate([cspread[t]] * (H // 128), 1)
                state = d * state + dx[row, lanes] * b
                decay = decay * d
                flow = flow + decay * (ocot[row, lanes] * c)
            return state, decay, flow

        zero = jnp.zeros((N, H), F32)
        state, decay, flow = lax.fori_loop(0, T // 8, steps, (zero, zero + 1.0, zero))
        for r in range(N // 8):
            for k in range(H // 128):
                at = r * 8 + h * (H // 128) + k
                part = (slice(8 * r, 8 * r + 8), slice(128 * k, 128 * k + 128))
                ends[at, 0] = state[part]
                ends[at, 1] = decay[part]
                ends[at + 16, 0] = flow[part]
                ends[at + 16, 1] = decay[part]
        return 0

    lax.fori_loop(0, C // H, half, 0)


def summary(pre, proj, wdelta, bias, dlog, gate, grad):
    full = jax.ShapeDtypeStruct((T, C), F32)
    wide = jax.ShapeDtypeStruct((T, N, 128), F32)
    return pl.pallas_call(
        summary_kernel,
        out_shape=(full, full, full, full, wide, wide, jax.ShapeDtypeStruct((CTX, 2, 8, 128), F32)),
        in_specs=[VMEM] * 7,
        out_specs=(VMEM,) * 7,
        compiler_params=pltpu.CompilerParams(vmem_limit_bytes=48 << 20),
        name="summary",
    )(pre, proj, wdelta, bias, dlog, gate, grad)


def border_kernel(ends, borders, got, back, ss, sr, bs, br):
    me = lax.axis_index("context")
    greet("context", CTX)
    pl.semaphore_wait(pltpu.get_barrier_semaphore(), CTX - 1)
    out = Exchange(ends, got, ss, sr, "context", CTX)
    out.start()
    got[me] = ends[me]
    out.wait_recv()
    backward = me // 16

    def follow(i, carried):
        at = i + backward * (CTX - 1 - 2 * i)
        back[at] = carried
        return got[at, 1] * carried + got[at, 0]

    lax.fori_loop(0, CTX, follow, jnp.zeros((8, 128), F32))
    home = Exchange(back, borders, bs, br, "context", CTX)
    home.start()
    borders[me] = back[me]
    home.wait_recv()
    out.wait_send()
    home.wait_send()


def border(ends):
    return pl.pallas_call(
        border_kernel,
        out_shape=jax.ShapeDtypeStruct((CTX, 8, 128), F32),
        in_specs=[VMEM],
        out_specs=VMEM,
        scratch_shapes=[
            pltpu.VMEM((CTX, 2, 8, 128), F32),
            pltpu.VMEM((CTX, 8, 128), F32),
        ] + [pltpu.SemaphoreType.DMA((CTX,))] * 4,
        compiler_params=pltpu.CompilerParams(collective_id=1, has_side_effects=True),
        name="border",
    )(ends)


def gradient_kernel(
    pre, proj, wdelta, dlog, skip, gate, grad, raw, deltas, dx, ocot, bspread, cspread, borders,
    gate_grad, direct, psel, dterm, prm,
    before, bblock, cblock, y, along, wsum, isum, osum, work, rates,
):
    flat = proj[...].reshape(T, WIDE)
    column = iota((128, 16 * N), 1)
    same = iota((T, 16 * N), 0) % 16 == column // N
    lane = iota((128, 16 * N), 0) % 64
    bblock[...] = jnp.where(
        same, dot_nn(flat[:, RANK:], (lane == column % N).astype(BF16)), 0.0
    ).astype(BF16)
    cblock[...] = jnp.where(
        same, dot_nn(flat[:, RANK:], (lane == column % N + N).astype(BF16)), 0.0
    ).astype(BF16)
    ones = (iota((16, 16 * N), 0) == iota((16, 16 * N), 1) // N).astype(BF16)
    wide = H // 128

    def edges(first, h):
        return jnp.concatenate(
            [
                jnp.concatenate([borders[first + r * 8 + h * wide + k] for k in range(wide)], 1)
                for r in range(N // 8)
            ],
            0,
        )

    def lane_sum(v):
        return functools.reduce(jnp.add, [v[:, 128 * k : 128 * k + 128] for k in range(wide)])

    def half(h, _):
        lanes = pl.ds(pl.multiple_of(h * H, H), H)
        rate = -jnp.exp(dlog[:, lanes])
        rate2 = rate * LOG2E

        def forward(block, state):
            for i in range(16):
                t = block * 16 + i
                row = pl.ds(t, 1)
                before[t] = state
                d = jnp.exp2(deltas[row, lanes] * rate2)
                b = jnp.concatenate([bspread[t]] * wide, 1)
                state = d * state + dx[row, lanes] * b
                work[N * i : N * i + N, :] = state.astype(BF16)
                osum[h, t] = lane_sum(state * ocot[row, lanes])
            rows = pl.ds(pl.multiple_of(block * 16, 16), 16)
            y[rows, lanes] = dot_nn(cblock[rows, :], work[...])
            return state

        lax.fori_loop(0, T // 16, forward, edges(0, h))

        def backward(index, carried):
            flow, total = carried
            block = T // 16 - 1 - index
            for i in reversed(range(16)):
                t = block * 16 + i
                row = pl.ds(t, 1)
                delta = deltas[row, lanes]
                c = jnp.concatenate([cspread[t]] * wide, 1)
                adjoint = ocot[row, lanes] * c + flow
                isum[h, t] = lane_sum(adjoint * dx[row, lanes])
                work[N * i : N * i + N, :] = adjoint.astype(BF16)
                flow = jnp.exp2(delta * rate2) * adjoint
                weighted = flow * before[t]
                total = total + weighted * delta
                rates[N * i : N * i + N, :] = (weighted * rate).astype(BF16)
            rows = pl.ds(pl.multiple_of(block * 16, 16), 16)
            along[rows, lanes] = dot_nn(bblock[rows, :], work[...])
            wsum[rows, lanes] = dot_nn(ones, rates[...])
            return flow, total

        _, total = lax.fori_loop(0, T // 16, backward, (edges(16, h), jnp.zeros((N, H), F32)))
        prm[0:N, lanes] = total * rate
        return 0

    lax.fori_loop(0, C // H, half, 0)

    v = pre[...]
    conv = v * sigmoid(v)
    cot = ocot[...]
    gain = skip[...]
    g = gate[...].astype(F32)
    outputs = y[...] + gain * conv
    gate_grad[...] = (grad[...].astype(F32) * outputs * silu_slope(g)).astype(BF16)
    near = along[...]
    direct[...] = gain * cot + deltas[...] * near
    raw_cot = (wsum[...] + conv * near) * sigmoid(raw[...])
    raw_half = raw_cot.astype(BF16)
    prm[N : N + 1, :] = jnp.sum(raw_cot, axis=0, keepdims=True)
    prm[N + 1 : N + 2, :] = jnp.sum(cot * conv, axis=0, keepdims=True)
    prm[N + 2 :, :] = jnp.zeros((6, C), F32)
    psel[:, :, :RANK] = dot_nn(raw_half, wdelta[...]).astype(BF16).reshape(TEN, ROWS, RANK)
    dterm[...] = dot_tn(flat[:, :RANK], raw_half).astype(BF16).reshape(CTX, RANK // CTX, C)

    unit = jnp.ones((128, 128), BF16)
    spot = iota((16 * N, 128), 1)
    which = iota((16 * N, 128), 0) % N

    def gather(block, _):
        rows = pl.ds(pl.multiple_of(block * 16, 16), 16)
        inputs = (isum[0, rows] + isum[1, rows]).reshape(16 * N, 128).astype(BF16)
        outs = (osum[0, rows] + osum[1, rows]).reshape(16 * N, 128).astype(BF16)
        both = jnp.where(spot == which, dot_nn(inputs, unit), 0.0) + jnp.where(
            spot == which + N, dot_nn(outs, unit), 0.0
        )
        psel[block, :, RANK:] = dot_nn(ones, both.astype(BF16)).astype(BF16)
        return 0

    lax.fori_loop(0, T // 16, gather, 0)


def gradient(*args):
    full = jax.ShapeDtypeStruct((T, C), F32)
    return pl.pallas_call(
        gradient_kernel,
        out_shape=(
            jax.ShapeDtypeStruct((T, C), BF16),
            full,
            jax.ShapeDtypeStruct((TEN, ROWS, WIDE), BF16),
            jax.ShapeDtypeStruct((CTX, RANK // CTX, C), BF16),
            jax.ShapeDtypeStruct((24, C), F32),
        ),
        in_specs=[VMEM] * 14,
        out_specs=(VMEM,) * 5,
        scratch_shapes=[
            pltpu.VMEM((T, N, H), F32),
            pltpu.VMEM((T, 16 * N), BF16),
            pltpu.VMEM((T, 16 * N), BF16),
            pltpu.VMEM((T, C), F32),
            pltpu.VMEM((T, C), F32),
            pltpu.VMEM((T, C), F32),
            pltpu.VMEM((2, T, N, 128), F32),
            pltpu.VMEM((2, T, N, 128), F32),
            pltpu.VMEM((16 * N, H), BF16),
            pltpu.VMEM((16 * N, H), BF16),
        ],
        compiler_params=pltpu.CompilerParams(vmem_limit_bytes=56 << 20),
        name="gradient",
    )(*args)


def back_kernel(
    psel, dterm, prm, pre, pad, direct, wsel, taps,
    inner_grad, sel_main, sel_extra, delta, params,
    got_sel, sel, got_d, main, got_m, extra, got_x, own, got_p, trail, edge, late,
    es, er, ts, tr, gs, gr, ds, dr, ms, mr, xs, xr, ps, pr, qs, qr,
):
    ctx, ten = lax.axis_index("context"), lax.axis_index("tensor")
    greet("tensor", TEN)
    greet("context", CTX)
    pl.semaphore_wait(pltpu.get_barrier_semaphore(), TEN - 1 + CTX - 1)

    scatter = Exchange(psel, got_sel, ts, tr, "tensor", TEN)
    scatter.start()
    deltas = Exchange(dterm, got_d, ds, dr, "context", CTX)
    deltas.start()
    got_sel[ten] = psel[ten]
    got_d[ctx] = dterm[ctx]
    value = pre[...]
    half = (value * sigmoid(value)).astype(BF16)
    target = iota((WIDE, WIDE), 0)
    source = iota((WIDE, WIDE), 1)
    order = jnp.where(target < RANK, target // 16 * 17 + target % 16, (target - RANK) * 17 + 16)
    order = ((order == source) & (target < PROJ)).astype(BF16)

    scatter.wait_recv()
    sel[ten] = jnp.sum(got_sel[...].astype(F32), axis=0).astype(BF16)
    gather = Exchange(sel, sel, gs, gr, "tensor", TEN, same=True)
    gather.start()
    gather.wait_recv()
    select_cot = sel[...].reshape(T, WIDE)

    turned = dot_nt(order, select_cot).astype(BF16)
    main[...] = dot_nn(turned[:RANK, :], half).astype(BF16).reshape(CTX, 16, C)
    mains = Exchange(main, got_m, ms, mr, "context", CTX)
    mains.start()
    got_m[ctx] = main[ctx]
    extra[...] = dot_nn(turned[RANK : RANK + CTX, :], half).reshape(CTX, 1, C)
    extras = Exchange(extra, got_x, xs, xr, "context", CTX)
    extras.start()
    got_x[ctx] = extra[ctx]

    cot = direct[...] + dot_nn(select_cot[:, :PROJ], wsel[...])
    cot = cot * silu_slope(value)
    trail[0:T, :] = cot
    edge[...] = cot[0:8, :]
    below = to_neighbour(edge, late, es, er, -1)
    below.start()
    rows = [prm[N : N + 2, :], jnp.sum(cot, axis=0, keepdims=True)]
    for k in range(TAPS):
        rows.append(
            jnp.sum(cot * pad[pl.ds(16 - TAPS + 1 + k, T), :], axis=0, keepdims=True)
        )
    rows.append(jnp.zeros((1, C), F32))
    rows = jnp.concatenate(rows, 0)
    for k in range(C // 128):
        lanes = slice(128 * k, 128 * k + 128)
        own[k] = prm[0:8, lanes]
        own[8 + k] = prm[8:16, lanes]
        own[16 + k] = rows[:, lanes]
        own[24 + k] = jnp.zeros((8, 128), F32)
    sums = Exchange(own, got_p, ps, pr, "context", CTX)
    sums.start()
    got_p[ctx] = own[ctx]

    below.wait()
    trail[T:, :] = late[...] * (ctx < CTX - 1).astype(F32)
    result = jnp.zeros((T, C), F32)
    for k in range(TAPS):
        result = result + taps[k : k + 1, :] * trail[pl.ds(TAPS - 1 - k, T), :]
    inner_grad[...] = result.astype(BF16)

    sums.wait_recv()
    params[ctx] = jnp.sum(got_p[...], axis=0)
    spreads = Exchange(params, params, qs, qr, "context", CTX, same=True)
    spreads.start()

    def add_up(ref, shape):
        return lax.fori_loop(
            0, CTX, lambda i, total: total + ref[i].astype(F32), jnp.zeros(shape, F32)
        )

    deltas.wait_recv()
    delta[...] = add_up(got_d, (16, C))
    extras.wait_recv()
    sel_extra[...] = add_up(got_x, (1, C))
    mains.wait_recv()
    sel_main[...] = add_up(got_m, (16, C))
    spreads.wait_recv()
    for exchange in (scatter, deltas, gather, mains, extras, sums, spreads):
        exchange.wait_send()


def back(*args):
    def pair(*shape):
        return [pltpu.VMEM(shape, BF16)]

    return pl.pallas_call(
        back_kernel,
        out_shape=(
            jax.ShapeDtypeStruct((T, C), BF16),
            jax.ShapeDtypeStruct((16, C), F32),
            jax.ShapeDtypeStruct((1, C), F32),
            jax.ShapeDtypeStruct((16, C), F32),
            jax.ShapeDtypeStruct((CTX, 8, 128), F32),
        ),
        in_specs=[VMEM] * 8,
        out_specs=(VMEM,) * 5,
        scratch_shapes=[
            pltpu.VMEM((TEN, ROWS, WIDE), BF16),
            pltpu.VMEM((TEN, ROWS, WIDE), BF16),
            pltpu.VMEM((CTX, 16, C), BF16),
            pltpu.VMEM((CTX, 16, C), BF16),
            pltpu.VMEM((CTX, 16, C), BF16),
            pltpu.VMEM((CTX, 1, C), F32),
            pltpu.VMEM((CTX, 1, C), F32),
            pltpu.VMEM((CTX, 8, 128), F32),
            pltpu.VMEM((CTX, 8, 128), F32),
            pltpu.VMEM((T + 8, C), F32),
            pltpu.VMEM((8, C), F32),
            pltpu.VMEM((8, C), F32),
            pltpu.SemaphoreType.DMA,
            pltpu.SemaphoreType.DMA,
        ]
        + [pltpu.SemaphoreType.DMA((TEN,))] * 4
        + [pltpu.SemaphoreType.DMA((CTX,))] * 10,
        compiler_params=pltpu.CompilerParams(
            collective_id=2, has_side_effects=True, vmem_limit_bytes=48 << 20
        ),
        name="back",
    )(*args)


def body(
    inner_in, gate_in, out_grad, kernel, kernel_shift, select_proj, delta_proj, delta_bias,
    decay_log, skip_gain,
):
    taps = kernel.T
    dlog = decay_log.T
    pad, pre, proj = front(inner_in, taps, kernel_shift[None], select_proj)
    raw, deltas, dx, ocot, bspread, cspread, ends = summary(
        pre, proj, delta_proj, delta_bias[None], dlog, gate_in, out_grad
    )
    borders = border(ends)
    gate_grad, direct, psel, dterm, prm = gradient(
        pre, proj, delta_proj, dlog, skip_gain[None], gate_in, out_grad,
        raw, deltas, dx, ocot, bspread, cspread, borders,
    )
    inner_grad, sel_main, sel_extra, delta, params = back(
        psel, dterm, prm, pre, pad, direct, select_proj, taps
    )
    rows = params.reshape(4, 8, 8, 128).transpose(0, 2, 1, 3).reshape(32, C)
    return (
        inner_grad,
        gate_grad,
        rows[19:23].T,
        rows[18],
        jnp.concatenate([sel_main, sel_extra], 0),
        delta.T,
        rows[16],
        rows[0:16].T,
        rows[17],
    )


def solution(mesh):
    return jax.shard_map(
        body,
        mesh=mesh,
        in_specs=(
            P("context", "tensor"),
            P("context", "tensor"),
            P("context", "tensor"),
            P("tensor", None),
            P("tensor"),
            P(None, "tensor"),
            P("tensor", None),
            P("tensor"),
            P("tensor", None),
            P("tensor"),
        ),
        out_specs=(
            P("context", "tensor"),
            P("context", "tensor"),
            P("tensor", None),
            P("tensor"),
            P("context", "tensor"),
            P("tensor", "context"),
            P("tensor"),
            P("tensor", None),
            P("tensor"),
        ),
        check_vma=False,
    )
```

```python
import functools

import jax
import jax.numpy as jnp
from jax import lax
from jax.experimental import pallas as pl
from jax.experimental.pallas import tpu as pltpu
from jax.sharding import PartitionSpec as P

N = 16
RANK = 512
TAPS = 4
PROJ = 544
WIDE = 640
T = 128
C = 1024
H = 512
CTX = 32
TEN = 8
ROWS = T // TEN
LOG2E = 1.4426950408889634
MESH = pl.DeviceIdType.MESH
F32 = jnp.float32
BF16 = jnp.bfloat16
VMEM = pl.BlockSpec(memory_space=pltpu.VMEM)


def dot_nn(a, b):
    return lax.dot_general(a, b, (((1,), (0,)), ((), ())), preferred_element_type=F32)


def dot_nt(a, b):
    return lax.dot_general(a, b, (((1,), (1,)), ((), ())), preferred_element_type=F32)


def dot_tn(a, b):
    return lax.dot_general(a, b, (((0,), (0,)), ((), ())), preferred_element_type=F32)


def iota(shape, axis):
    return lax.broadcasted_iota(jnp.int32, shape, axis)


def sigmoid(v):
    return jax.nn.sigmoid(v)


def silu_slope(v):
    s = sigmoid(v)
    return s * (1.0 + v * (1.0 - s))


def split_tile(v):
    high = v.astype(BF16).astype(F32)
    return jnp.where(iota(v.shape, 1) < 64, high, v - high).astype(BF16)


class Exchange:
    def __init__(self, src, dst, sems, axis, size, same=False, chips=False):
        self.src, self.dst, self.send, self.recv = src, dst, sems[0], sems[1]
        self.axis, self.size, self.same, self.chips = axis, size, same, chips

    def copy(self, off):
        me = lax.axis_index(self.axis)
        at = me // 2 if self.chips else me
        peer = lax.rem(at + off, self.size)
        return pltpu.make_async_remote_copy(
            src_ref=self.src.at[at] if self.same else self.src.at[peer],
            dst_ref=self.dst.at[at],
            send_sem=self.send.at[off],
            recv_sem=self.recv.at[off],
            device_id={self.axis: peer * 2 + lax.rem(me, 2) if self.chips else peer},
            device_id_type=MESH,
        )

    def start(self):
        lax.fori_loop(1, self.size, lambda off, _: (self.copy(off).start(), 0)[1], 0)

    def wait_recv(self):
        lax.fori_loop(1, self.size, lambda off, _: (self.copy(off).wait_recv(), 0)[1], 0)

    def wait_send(self):
        lax.fori_loop(1, self.size, lambda off, _: (self.copy(off).wait_send(), 0)[1], 0)


def greet(axis, size):
    me = lax.axis_index(axis)
    barrier = pltpu.get_barrier_semaphore()

    def signal(off, _):
        pl.semaphore_signal(
            barrier, inc=1, device_id={axis: lax.rem(me + off, size)}, device_id_type=MESH
        )
        return 0

    lax.fori_loop(1, size, signal, 0)


def to_neighbour(src, dst, send, recv, step):
    peer = lax.rem(lax.axis_index("context") + step + CTX, CTX)
    return pltpu.make_async_remote_copy(
        src_ref=src, dst_ref=dst, send_sem=send, recv_sem=recv,
        device_id={"context": peer}, device_id_type=MESH,
    )


def spread(tile, first):
    rows = T * N
    repeat = (iota((rows, T), 0) // N == iota((rows, T), 1)).astype(BF16)
    each = dot_nn(repeat, tile)
    mine = iota((rows, 128), 1) % 64 == iota((rows, 128), 0) % N + first
    return dot_nn(jnp.where(mine, each, 0.0).astype(BF16), jnp.ones((128, 128), BF16))


CHIPS = CTX // 2
HALVES = C // H
LT = H // 128

SCRATCH = (
    ("pad", (T + 16, C), F32),
    ("pre", (T, C), F32),
    ("conv", (T, C), F32),
    ("slope", (T, C), F32),
    ("half", (T, C), BF16),
    ("ocot", (T, C), F32),
    ("gslope", (T, C), F32),
    ("sig", (T, C), F32),
    ("deltas", (T, C), F32),
    ("dx", (T, C), F32),
    ("y", (T, C), F32),
    ("along", (T, C), F32),
    ("wsum", (T, C), F32),
    ("direct", (T, C), F32),
    ("halo", (16, C), BF16),
    ("wtail", (128, C), BF16),
    ("part", (TEN, ROWS, WIDE), BF16),
    ("got_part", (TEN, ROWS, WIDE), BF16),
    ("proj", (TEN, ROWS, WIDE), BF16),
    ("bspread", (T, N, 128), F32),
    ("cspread", (T, N, 128), F32),
    ("bblock", (T, 16 * N), BF16),
    ("cblock", (T, 16 * N), BF16),
    ("steps", (CTX, 8, 128), F32),
    ("ends", (CTX, 8, 128), F32),
    ("got_ends", (CTX, 8, 128), F32),
    ("decays", (CTX, 8, 128), F32),
    ("back", (CTX, 8, 128), F32),
    ("borders", (CTX, 8, 128), F32),
    ("before", (T, N, H), F32),
    ("isum", (HALVES, T, N, 128), F32),
    ("osum", (HALVES, T, N, 128), F32),
    ("work", (16 * N, H), BF16),
    ("rates", (16 * N, H), BF16),
    ("decay_part", (N, C), F32),
    ("psel", (TEN, ROWS, WIDE), BF16),
    ("got_psel", (TEN, ROWS, WIDE), BF16),
    ("sel", (TEN, ROWS, WIDE), BF16),
    ("order", (WIDE, WIDE), BF16),
    ("dterm", (2, CHIPS, 16, C), BF16),
    ("dpair", (CHIPS, 16, C), BF16),
    ("dsum", (CHIPS, 16, C), BF16),
    ("got_d", (CHIPS, 16, C), BF16),
    ("mterm", (2, CHIPS, 16, C), BF16),
    ("mpair", (CHIPS, 16, C), BF16),
    ("msum", (CHIPS, 16, C), BF16),
    ("got_m", (CHIPS, 16, C), BF16),
    ("own", (CTX, 2, 8, 128), F32),
    ("got_own", (CTX, 2, 8, 128), F32),
    ("trail", (T + 8, C), F32),
    ("edge", (8, C), F32),
    ("late", (8, C), F32),
)
INPUTS = (
    ("inner", (T, C), BF16),
    ("gate", (T, C), BF16),
    ("grad", (T, C), BF16),
    ("taps", (TAPS, C), F32),
    ("shift", (1, C), F32),
    ("wsel", (PROJ, C), BF16),
    ("wdelta", (C, RANK), BF16),
    ("bias", (1, C), F32),
    ("dlog", (N, C), F32),
    ("skip", (1, C), F32),
)
OUTPUTS = (
    ("inner_grad", (T, C), BF16),
    ("gate_grad", (T, C), BF16),
    ("sel_main", (16, C), F32),
    ("sel_extra", (8, 128), F32),
    ("delta_grad", (16, C), F32),
    ("params", (CTX, 8, 128), F32),
)
SEMS = (
    ("in", (len(INPUTS),)),
    ("halo", (2,)),
    ("part", (2, TEN)),
    ("proj", (2, TEN)),
    ("steps", (2, CTX)),
    ("ends", (2, CTX)),
    ("back", (2, CTX)),
    ("psel", (2, TEN)),
    ("sel", (2, TEN)),
    ("dpair", (2,)),
    ("dsum", (2, CHIPS)),
    ("mpair", (2,)),
    ("msum", (2, CHIPS)),
    ("own", (2, CTX)),
    ("params", (2, CTX)),
    ("edge", (2,)),
)


class Refs:
    pass


def tile_of(v, r, k):
    return v[8 * r : 8 * r + 8, 128 * k : 128 * k + 128]


def wide_of(v):
    return jnp.concatenate([v] * LT, 1)


def lane_sum(v):
    return functools.reduce(jnp.add, [v[:, 128 * k : 128 * k + 128] for k in range(LT)])


def half_lanes(h):
    return pl.ds(pl.multiple_of(h * H, H), H)


def rows_of(block):
    return pl.ds(pl.multiple_of(block * 16, 16), 16)


def convolve(z, first, rows):
    value = jnp.zeros((rows, C), F32) + z.shift[...]
    for k in range(TAPS):
        value = value + z.taps[k : k + 1, :] * z.pad[pl.ds(first + 16 - TAPS + 1 + k, rows), :]
    z.pre[pl.ds(first, rows), :] = value
    s = sigmoid(value)
    conv = value * s
    z.conv[pl.ds(first, rows), :] = conv
    z.half[pl.ds(first, rows), :] = conv.astype(BF16)
    z.slope[pl.ds(first, rows), :] = s * (1.0 + value * (1.0 - s))


def project(z, first, rows):
    half = z.half[pl.ds(first, rows), :]
    blocks = pl.ds(first // ROWS, rows // ROWS)
    shape = (rows // ROWS, ROWS)
    z.part[blocks, :, :RANK] = dot_nt(half, z.wsel[:RANK, :]).astype(BF16).reshape(*shape, RANK)
    z.part[blocks, :, RANK:] = split_tile(dot_nt(half, z.wtail[...])).reshape(*shape, 128)


def summarize(z):
    def half(h, _):
        lanes = half_lanes(h)
        rate = jnp.exp(z.dlog[:, lanes]) * (-LOG2E)

        def steps(block, carried):
            state, decay, flow = carried
            for i in range(8):
                t = block * 8 + i
                row = pl.ds(t, 1)
                d = jnp.exp2(z.deltas[row, lanes] * rate)
                state = d * state + z.dx[row, lanes] * wide_of(z.bspread[t])
                decay = decay * d
                flow = flow + decay * (z.ocot[row, lanes] * wide_of(z.cspread[t]))
            return state, decay, flow

        zero = jnp.zeros((N, H), F32)
        state, _, flow = lax.fori_loop(0, T // 8, steps, (zero, zero + 1.0, zero))
        for r in range(N // 8):
            for k in range(LT):
                at = r * 8 + h * LT + k
                z.ends[at] = tile_of(state, r, k)
                z.ends[at + 16] = tile_of(flow, r, k)
        return 0

    lax.fori_loop(0, HALVES, half, 0)


def recur(z):
    ones = (iota((16, 16 * N), 0) == iota((16, 16 * N), 1) // N).astype(BF16)

    def edges(first, h):
        return jnp.concatenate(
            [
                jnp.concatenate([z.borders[first + r * 8 + h * LT + k] for k in range(LT)], 1)
                for r in range(N // 8)
            ],
            0,
        )

    def half(h, _):
        lanes = half_lanes(h)
        rate = -jnp.exp(z.dlog[:, lanes])
        rate2 = rate * LOG2E

        def forward(block, state):
            for i in range(16):
                t = block * 16 + i
                row = pl.ds(t, 1)
                z.before[t] = state
                d = jnp.exp2(z.deltas[row, lanes] * rate2)
                state = d * state + z.dx[row, lanes] * wide_of(z.bspread[t])
                z.work[N * i : N * i + N, :] = state.astype(BF16)
                z.osum[h, t] = lane_sum(state * z.ocot[row, lanes])
            rows = rows_of(block)
            z.y[rows, lanes] = dot_nn(z.cblock[rows, :], z.work[...])
            return state

        lax.fori_loop(0, T // 16, forward, edges(0, h))

        def backward(index, carried):
            flow, total = carried
            block = T // 16 - 1 - index
            for i in reversed(range(16)):
                t = block * 16 + i
                row = pl.ds(t, 1)
                delta = z.deltas[row, lanes]
                adjoint = z.ocot[row, lanes] * wide_of(z.cspread[t]) + flow
                z.isum[h, t] = lane_sum(adjoint * z.dx[row, lanes])
                z.work[N * i : N * i + N, :] = adjoint.astype(BF16)
                flow = jnp.exp2(delta * rate2) * adjoint
                weighted = flow * z.before[t]
                total = total + weighted * delta
                z.rates[N * i : N * i + N, :] = (weighted * rate).astype(BF16)
            rows = rows_of(block)
            z.along[rows, lanes] = dot_nn(z.bblock[rows, :], z.work[...])
            z.wsum[rows, lanes] = dot_nn(ones, z.rates[...])
            return flow, total

        _, total = lax.fori_loop(0, T // 16, backward, (edges(16, h), jnp.zeros((N, H), F32)))
        z.decay_part[:, lanes] = total * rate
        return 0

    lax.fori_loop(0, HALVES, half, 0)

    unit = jnp.ones((128, 128), BF16)
    spot = iota((16 * N, 128), 1)
    which = iota((16 * N, 128), 0) % N

    def gather(block, _):
        rows = rows_of(block)
        inputs = functools.reduce(jnp.add, [z.isum[h, rows] for h in range(HALVES)])
        outs = functools.reduce(jnp.add, [z.osum[h, rows] for h in range(HALVES)])
        both = jnp.where(
            spot == which, dot_nn(inputs.reshape(16 * N, 128).astype(BF16), unit), 0.0
        ) + jnp.where(
            spot == which + N, dot_nn(outs.reshape(16 * N, 128).astype(BF16), unit), 0.0
        )
        z.psel[block, :, RANK:] = dot_nn(ones, both.astype(BF16)).astype(BF16)
        return 0

    lax.fori_loop(0, T // 16, gather, 0)


def to_sibling(src, dst, sems):
    me = lax.axis_index("context")
    return pltpu.make_async_remote_copy(
        src_ref=src, dst_ref=dst, send_sem=sems.at[0], recv_sem=sems.at[1],
        device_id={"context": me + 1 - 2 * lax.rem(me, 2)}, device_id_type=MESH,
    )


def layer_kernel(*refs):
    z, given, sem = Refs(), Refs(), Refs()
    refs = list(refs)
    for name, _, _ in INPUTS:
        setattr(given, name, refs.pop(0))
    for name, _, _ in OUTPUTS + INPUTS + SCRATCH:
        setattr(z, name, refs.pop(0))
    for name, _ in SEMS:
        setattr(sem, name, refs.pop(0))
    ctx, ten = lax.axis_index("context"), lax.axis_index("tensor")
    chip, core = ctx // 2, lax.rem(ctx, 2)

    loads = {}
    for i, (name, _, _) in enumerate(INPUTS):
        loads[name] = pltpu.make_async_copy(
            getattr(given, name), getattr(z, name), getattr(sem, "in").at[i]
        )

    for name in ("inner", "taps", "shift", "wsel", "gate", "grad", "dlog", "wdelta", "bias", "skip"):
        loads[name].start()
    greet("tensor", TEN)
    greet("context", CTX)

    for name in ("inner", "taps", "shift"):
        loads[name].wait()
    z.pad[16:, :] = z.inner[...].astype(F32)
    convolve(z, 16, T - 16)
    pl.semaphore_wait(pltpu.get_barrier_semaphore(), TEN - 1 + CTX - 1)
    halo = to_neighbour(z.inner.at[pl.ds(T - 16, 16)], z.halo, sem.halo.at[0], sem.halo.at[1], 1)
    halo.start()
    loads["wsel"].wait()
    tail = z.wsel[RANK:PROJ, :]
    z.wtail[0:32, :] = tail
    z.wtail[32:64, :] = jnp.zeros((32, C), BF16)
    z.wtail[64:96, :] = tail
    z.wtail[96:128, :] = jnp.zeros((32, C), BF16)
    project(z, 16, T - 16)
    halo.wait()
    z.pad[0:16, :] = z.halo[...].astype(F32) * (ctx > 0).astype(F32)
    convolve(z, 0, 16)
    project(z, 0, 16)
    scatter = Exchange(z.part, z.got_part, (sem.part.at[0], sem.part.at[1]), "tensor", TEN)
    scatter.start()
    z.got_part[ten] = z.part[ten]

    loads["gate"].wait()
    loads["grad"].wait()
    g = z.gate[...].astype(F32)
    s = sigmoid(g)
    grad = z.grad[...].astype(F32)
    z.ocot[...] = grad * (g * s)
    z.gslope[...] = grad * (s * (1.0 + g * (1.0 - s)))

    scatter.wait_recv()
    total = jnp.sum(z.got_part[...].astype(F32), axis=0)
    bc = total[:, RANK:]
    bc = bc + pltpu.roll(bc, 64, 1)
    z.proj[ten, :, :RANK] = total[:, :RANK].astype(BF16)
    z.proj[ten, :, RANK:] = split_tile(bc)
    gather = Exchange(
        z.proj, z.proj, (sem.proj.at[0], sem.proj.at[1]), "tensor", TEN, same=True
    )
    gather.start()
    target = iota((WIDE, WIDE), 0)
    source = iota((WIDE, WIDE), 1)
    place = target % 256
    order = jnp.where(
        target < RANK,
        (place // 16 * 2 + target // 256) * 17 + place % 16,
        (target - RANK) * 17 + 16,
    )
    z.order[...] = ((order == source) & (target < PROJ)).astype(BF16)
    for name in ("dlog", "wdelta", "bias", "skip"):
        loads[name].wait()
    gather.wait_recv()

    flat = z.proj[...].reshape(T, WIDE)
    raw = dot_nt(flat[:, :RANK], z.wdelta[...]) + z.bias[...]
    step = jnp.maximum(raw, 0.0) + jnp.log1p(jnp.exp(-jnp.abs(raw)))
    z.deltas[...] = step
    lengths = jnp.sum(step, axis=0, keepdims=True)
    for k in range(8):
        z.steps[ctx, k : k + 1, :] = lengths[:, 128 * k : 128 * k + 128]
    steps = Exchange(
        z.steps, z.steps, (sem.steps.at[0], sem.steps.at[1]), "context", CTX, same=True
    )
    steps.start()
    z.sig[...] = sigmoid(raw)
    z.dx[...] = step * z.conv[...]
    z.bspread[...] = spread(flat[:, RANK:], 0).reshape(T, N, 128)
    z.cspread[...] = spread(flat[:, RANK:], N).reshape(T, N, 128)
    summarize(z)

    ends = Exchange(z.ends, z.got_ends, (sem.ends.at[0], sem.ends.at[1]), "context", CTX)
    ends.start()
    z.got_ends[ctx] = z.ends[ctx]
    backward = ctx // 16
    at_row = pl.ds(pl.multiple_of(lax.rem(ctx, 16) // 8 * 8, 8), 8)
    at_lane = lax.rem(ctx, 8)
    rate = jnp.exp(z.dlog[at_row, pl.ds(pl.multiple_of(at_lane * 128, 128), 128)]) * (-LOG2E)
    steps.wait_recv()

    def shrink(i, _):
        z.decays[i] = jnp.exp2(rate * z.steps[i, pl.ds(at_lane, 1), :])
        return 0

    lax.fori_loop(0, CTX, shrink, 0)
    column = iota((128, 16 * N), 1)
    same = iota((T, 16 * N), 0) % 16 == column // N
    lane = iota((128, 16 * N), 0) % 64
    z.bblock[...] = jnp.where(
        same, dot_nn(flat[:, RANK:], (lane == column % N).astype(BF16)), 0.0
    ).astype(BF16)
    z.cblock[...] = jnp.where(
        same, dot_nn(flat[:, RANK:], (lane == column % N + N).astype(BF16)), 0.0
    ).astype(BF16)
    ends.wait_recv()

    def follow(i, carried):
        at = i + backward * (CTX - 1 - 2 * i)
        z.back[at] = carried
        return z.decays[at] * carried + z.got_ends[at]

    lax.fori_loop(0, CTX, follow, jnp.zeros((8, 128), F32))
    home = Exchange(z.back, z.borders, (sem.back.at[0], sem.back.at[1]), "context", CTX)
    home.start()
    z.borders[ctx] = z.back[ctx]
    home.wait_recv()

    recur(z)

    near = z.along[...]
    raw_cot = (z.wsum[...] + z.conv[...] * near) * z.sig[...]
    raw_half = raw_cot.astype(BF16)
    z.psel[:, :, :RANK] = dot_nn(raw_half, z.wdelta[...]).astype(BF16).reshape(TEN, ROWS, RANK)
    scatter2 = Exchange(z.psel, z.got_psel, (sem.psel.at[0], sem.psel.at[1]), "tensor", TEN)
    scatter2.start()
    z.got_psel[ten] = z.psel[ten]

    term = dot_tn(flat[:, :RANK], raw_half).astype(BF16).reshape(CHIPS, 2, 16, C)
    z.dterm[0] = term[:, 0]
    z.dterm[1] = term[:, 1]
    dpair = to_sibling(z.dterm.at[1 - core], z.dpair, sem.dpair)
    dpair.start()
    cot = z.ocot[...]
    gain = z.skip[...]
    z.gate_grad[...] = (z.gslope[...] * (z.y[...] + gain * z.conv[...])).astype(BF16)
    z.direct[...] = gain * cot + z.deltas[...] * near
    early = [
        jnp.sum(raw_cot, axis=0, keepdims=True),
        jnp.sum(cot * z.conv[...], axis=0, keepdims=True),
    ]
    dpair.wait()
    z.dsum[...] = (z.dterm[core].astype(F32) + z.dpair[...].astype(F32)).astype(BF16)
    deltas = Exchange(
        z.dsum, z.got_d, (sem.dsum.at[0], sem.dsum.at[1]), "context", CHIPS, chips=True
    )
    deltas.start()
    z.got_d[chip] = z.dsum[chip]

    scatter2.wait_recv()
    z.sel[ten] = jnp.sum(z.got_psel[...].astype(F32), axis=0).astype(BF16)
    gather2 = Exchange(z.sel, z.sel, (sem.sel.at[0], sem.sel.at[1]), "tensor", TEN, same=True)
    gather2.start()
    gather2.wait_recv()
    select_cot = z.sel[...].reshape(T, WIDE)

    turned = dot_nt(z.order[...], select_cot).astype(BF16)
    z.mterm[...] = dot_nn(turned[:RANK, :], z.half[...]).astype(BF16).reshape(2, CHIPS, 16, C)
    mpair = to_sibling(z.mterm.at[1 - core], z.mpair, sem.mpair)
    mpair.start()
    extra = dot_nn(turned[RANK : RANK + CTX, :], z.half[...])
    for k in range(8):
        z.own[:, 1, k, :] = extra[:, 128 * k : 128 * k + 128]
    pre_cot = (z.direct[...] + dot_nn(select_cot[:, :PROJ], z.wsel[...])) * z.slope[...]
    z.trail[0:T, :] = pre_cot
    z.edge[...] = pre_cot[0:8, :]
    below = to_neighbour(z.edge, z.late, sem.edge.at[0], sem.edge.at[1], -1)
    below.start()
    mpair.wait()
    z.msum[...] = (z.mterm[core].astype(F32) + z.mpair[...].astype(F32)).astype(BF16)
    mains = Exchange(
        z.msum, z.got_m, (sem.msum.at[0], sem.msum.at[1]), "context", CHIPS, chips=True
    )
    mains.start()
    z.got_m[chip] = z.msum[chip]

    late = [jnp.sum(pre_cot, axis=0, keepdims=True)]
    for k in range(TAPS):
        late.append(
            jnp.sum(pre_cot * z.pad[pl.ds(16 - TAPS + 1 + k, T), :], axis=0, keepdims=True)
        )
    rows = jnp.concatenate(early + late + [jnp.zeros((1, C), F32)], 0)
    for k in range(8):
        lanes = slice(128 * k, 128 * k + 128)
        z.own[k, 0] = z.decay_part[0:8, lanes]
        z.own[8 + k, 0] = z.decay_part[8:16, lanes]
        z.own[16 + k, 0] = rows[:, lanes]
        z.own[24 + k, 0] = jnp.zeros((8, 128), F32)
    sums = Exchange(z.own, z.got_own, (sem.own.at[0], sem.own.at[1]), "context", CTX)
    sums.start()
    z.got_own[ctx] = z.own[ctx]

    below.wait()
    z.trail[T:, :] = z.late[...] * (ctx < CTX - 1).astype(F32)
    result = jnp.zeros((T, C), F32)
    for k in range(TAPS):
        result = result + z.taps[k : k + 1, :] * z.trail[pl.ds(TAPS - 1 - k, T), :]
    z.inner_grad[...] = result.astype(BF16)
    deltas.wait_recv()
    z.delta_grad[...] = jnp.sum(z.got_d[...].astype(F32), axis=0)

    sums.wait_recv()
    z.params[ctx] = jnp.sum(z.got_own[:, 0], axis=0)
    spreads = Exchange(
        z.params, z.params, (sem.params.at[0], sem.params.at[1]), "context", CTX, same=True
    )
    spreads.start()
    z.sel_extra[...] = jnp.sum(z.got_own[:, 1], axis=0)
    mains.wait_recv()
    z.sel_main[...] = jnp.sum(z.got_m[...].astype(F32), axis=0)
    spreads.wait_recv()
    for exchange in (scatter, gather, steps, ends, home, scatter2, deltas, gather2, mains, sums, spreads):
        exchange.wait_send()


def layer(*args):
    return pl.pallas_call(
        layer_kernel,
        out_shape=[jax.ShapeDtypeStruct(shape, kind) for _, shape, kind in OUTPUTS],
        in_specs=[pl.BlockSpec(memory_space=pl.ANY)] * len(INPUTS),
        out_specs=[VMEM] * len(OUTPUTS),
        scratch_shapes=[pltpu.VMEM(shape, kind) for _, shape, kind in INPUTS + SCRATCH]
        + [pltpu.SemaphoreType.DMA(shape) for _, shape in SEMS],
        compiler_params=pltpu.CompilerParams(
            collective_id=0, has_side_effects=True, vmem_limit_bytes=56 << 20
        ),
        name="layer",
    )(*args)


def finish_kernel(
    inner_grad, gate_grad, sel_main, sel_extra, delta, params,
    inner_out, gate_out, taps_out, shift_out, sel_out, delta_out, bias_out, decay_out, skip_out,
):
    inner_out[...] = inner_grad[...]
    gate_out[...] = gate_grad[...]
    sel_out[0:16, :] = sel_main[...]
    delta_out[...] = delta[...]
    for k in range(8):
        lanes = slice(128 * k, 128 * k + 128)
        sel_out[16:17, lanes] = sel_extra[k : k + 1, :]
        decay_out[0:8, lanes] = params[k]
        decay_out[8:16, lanes] = params[8 + k]
        rows = params[16 + k]
        bias_out[:, lanes] = rows[0:1, :]
        skip_out[:, lanes] = rows[1:2, :]
        shift_out[:, lanes] = rows[2:3, :]
        taps_out[:, lanes] = rows[3:7, :]


def finish(*args):
    shapes = ((T, C), (T, C), (TAPS, C), (1, C), (17, C), (16, C), (1, C), (N, C), (1, C))
    return pl.pallas_call(
        finish_kernel,
        out_shape=[
            jax.ShapeDtypeStruct(shape, BF16 if i < 2 else F32) for i, shape in enumerate(shapes)
        ],
        in_specs=[VMEM] * 6,
        out_specs=[VMEM] * 9,
        name="finish",
    )(*args)


def body(
    inner_in, gate_in, out_grad, kernel, kernel_shift, select_proj, delta_proj, delta_bias,
    decay_log, skip_gain,
):
    parts = layer(
        inner_in, gate_in, out_grad, kernel.T, kernel_shift[None], select_proj, delta_proj,
        delta_bias[None], decay_log.T, skip_gain[None],
    )
    inner_grad, gate_grad, taps, shift, select, delta, bias, decay, skip = finish(*parts)
    return (
        inner_grad, gate_grad, taps.T, shift[0], select, delta.T, bias[0], decay.T, skip[0],
    )


def solution(mesh):
    return jax.shard_map(
        body,
        mesh=mesh,
        in_specs=(
            P("context", "tensor"),
            P("context", "tensor"),
            P("context", "tensor"),
            P("tensor", None),
            P("tensor"),
            P(None, "tensor"),
            P("tensor", None),
            P("tensor"),
            P("tensor", None),
            P("tensor"),
        ),
        out_specs=(
            P("context", "tensor"),
            P("context", "tensor"),
            P("tensor", None),
            P("tensor"),
            P("context", "tensor"),
            P("tensor", "context"),
            P("tensor"),
            P("tensor", None),
            P("tensor"),
        ),
        check_vma=False,
    )
```

```python
import functools

import jax
import jax.numpy as jnp
from jax import lax
from jax.experimental import pallas as pl
from jax.experimental.pallas import tpu as pltpu
from jax.sharding import PartitionSpec as P

N = 16
RANK = 512
TAPS = 4
PROJ = 544
WIDE = 640
T = 128
C = 1024
H = 512
CTX = 32
TEN = 8
CHIPS = CTX // 2
ROWS = T // TEN
LOG2E = 1.4426950408889634
MESH = pl.DeviceIdType.MESH
F32 = jnp.float32
BF16 = jnp.bfloat16
VMEM = pl.BlockSpec(memory_space=pltpu.VMEM)


def dot_nn(a, b):
    return lax.dot_general(a, b, (((1,), (0,)), ((), ())), preferred_element_type=F32)


def dot_nt(a, b):
    return lax.dot_general(a, b, (((1,), (1,)), ((), ())), preferred_element_type=F32)


def dot_tn(a, b):
    return lax.dot_general(a, b, (((0,), (0,)), ((), ())), preferred_element_type=F32)


def iota(shape, axis):
    return lax.broadcasted_iota(jnp.int32, shape, axis)


def sigmoid(v):
    return jax.nn.sigmoid(v)


def silu_slope(v):
    s = sigmoid(v)
    return s * (1.0 + v * (1.0 - s))


def split_tile(v):
    high = v.astype(BF16).astype(F32)
    return jnp.where(iota(v.shape, 1) < 64, high, v - high).astype(BF16)


def far_first(k, size):
    return size // 2 + (k + 1) // 2 * (1 - 2 * lax.rem(k, 2))


class Exchange:
    def __init__(self, src, dst, sems, group, same=False):
        self.src, self.dst, self.send, self.recv = src, dst, sems.at[0], sems.at[1]
        self.group, self.same = group, same
        self.count = {"tensor": TEN, "context": CTX, "chips": CHIPS}[group] - 1

    def copy(self, k):
        if self.group == "tensor":
            at = lax.axis_index("tensor")
            peer = lax.rem(at + far_first(k, TEN), TEN)
            target = {"tensor": peer}
        else:
            me = lax.axis_index("context")
            place, core = (k // 2, 1 - lax.rem(k, 2)) if self.group == "context" else (k, 0)
            x = lax.rem(me // 8 + far_first(place // 4, 4), 4)
            y = lax.rem(me // 2 + far_first(lax.rem(place, 4), 4), 4)
            peer = (x * 4 + y) * 2 + lax.rem(me + core, 2)
            target = {"context": peer}
            at = me
            if self.group == "chips":
                at, peer = me // 2, peer // 2
        return self.made(at, peer, k, target)

    def made(self, at, peer, k, target):
        return pltpu.make_async_remote_copy(
            src_ref=self.src.at[at] if self.same else self.src.at[peer],
            dst_ref=self.dst.at[at],
            send_sem=self.send.at[k],
            recv_sem=self.recv.at[k],
            device_id=target,
            device_id_type=MESH,
        )

    def every(self, act):
        lax.fori_loop(0, self.count, lambda k, _: (act(self.copy(k)), 0)[1], 0)

    def start(self):
        self.every(lambda copy: copy.start())

    def wait_recv(self):
        self.every(lambda copy: copy.wait_recv())

    def wait_send(self):
        self.every(lambda copy: copy.wait_send())

    def to_core(self, core, act):
        other = lax.rem(lax.axis_index("context") + core, 2)
        lax.fori_loop(
            0, CHIPS - 1 + other, lambda q, _: (act(self.copy(2 * q + 1 - other)), 0)[1], 0
        )


class ToEighth(Exchange):
    def __init__(self, src, dst, sems, back=False):
        super().__init__(src, dst, sems, "context")
        self.back = back

    def made(self, at, peer, k, target):
        return pltpu.make_async_remote_copy(
            src_ref=self.src.at[at // 4 if self.back else peer // 4],
            dst_ref=self.dst.at[at // 4 if self.back else at],
            send_sem=self.send.at[k],
            recv_sem=self.recv.at[k],
            device_id=target,
            device_id_type=MESH,
        )

    def few(self, act):
        me = lax.axis_index("context")
        odd = lax.rem(me // 2, 2)

        def one(m, _):
            b = lax.rem(m, 2) * (3 - 2 * odd) + odd
            act(self.copy(2 * (m // 2 * 4 + b) + 1 - lax.rem(me, 2)))
            return 0

        lax.fori_loop(0, 8 - lax.rem(me + 3, 4) // 3, one, 0)

    def all(self, act):
        @pl.when(lax.rem(lax.axis_index("context"), 4) == 0)
        def _():
            self.every(act)

    def start(self):
        (self.all if self.back else self.few)(lambda copy: copy.start())

    def wait_recv(self):
        (self.few if self.back else self.all)(lambda copy: copy.wait_recv())

    def wait_send(self):
        (self.all if self.back else self.few)(lambda copy: copy.wait_send())


def greet(axis, size):
    me = lax.axis_index(axis)
    barrier = pltpu.get_barrier_semaphore()

    def signal(off, _):
        pl.semaphore_signal(
            barrier, inc=1, device_id={axis: lax.rem(me + off, size)}, device_id_type=MESH
        )
        return 0

    lax.fori_loop(1, size, signal, 0)


def to_neighbour(src, dst, send, recv, step):
    peer = lax.rem(lax.axis_index("context") + step + CTX, CTX)
    return pltpu.make_async_remote_copy(
        src_ref=src, dst_ref=dst, send_sem=send, recv_sem=recv,
        device_id={"context": peer}, device_id_type=MESH,
    )


def spread(z, tile):
    rows = T * N
    repeat = (iota((rows, T), 0) // N == iota((rows, T), 1)).astype(BF16)
    each = dot_nn(repeat, tile)
    place = iota((rows, 128), 1) % 64 - iota((rows, 128), 0) % N
    unit = jnp.ones((128, 128), BF16)
    z.bspread[...] = dot_nn(jnp.where(place == 0, each, 0.0).astype(BF16), unit).reshape(T, N, 128)
    z.cspread[...] = dot_nn(jnp.where(place == N, each, 0.0).astype(BF16), unit).reshape(T, N, 128)


HALVES = C // H
LT = H // 128

SCRATCH = (
    ("pad", (T + 16, C), F32),
    ("pre", (T, C), F32),
    ("conv", (T, C), F32),
    ("slope", (T, C), F32),
    ("half", (T, C), BF16),
    ("ocot", (T, C), F32),
    ("gslope", (T, C), F32),
    ("sig", (T, C), F32),
    ("deltas", (T, C), F32),
    ("dx", (T, C), F32),
    ("y", (T + 16, C), F32),
    ("along", (T + 16, C), F32),
    ("wsum", (T + 16, C), F32),
    ("direct", (T, C), F32),
    ("halo", (16, C), BF16),
    ("wtail", (128, C), BF16),
    ("part", (TEN, ROWS, WIDE), BF16),
    ("got_part", (TEN, ROWS, WIDE), BF16),
    ("proj", (TEN, ROWS, WIDE), BF16),
    ("bspread", (T, N, 128), F32),
    ("cspread", (T, N, 128), F32),
    ("bblock", (T, 16 * N), BF16),
    ("cblock", (T, 16 * N), BF16),
    ("steps", (CTX, 8, 128), F32),
    ("ends", (CTX, 8, 128), F32),
    ("got_ends", (CTX, 8, 128), F32),
    ("decays", (CTX, 8, 128), F32),
    ("back", (CTX, 8, 128), F32),
    ("borders", (CTX, 8, 128), F32),
    ("before", (T, N, H), F32),
    ("isum", (HALVES, T, N, 128), F32),
    ("osum", (HALVES, T, N, 128), F32),
    ("work0", (16 * N, H), BF16),
    ("work1", (16 * N, H), BF16),
    ("rates0", (16 * N, H), BF16),
    ("rates1", (16 * N, H), BF16),
    ("decay_part", (N, C), F32),
    ("psel", (TEN, ROWS, WIDE), BF16),
    ("got_psel", (TEN, ROWS, WIDE), BF16),
    ("sel", (TEN, ROWS, WIDE), BF16),
    ("order", (WIDE, WIDE), BF16),
    ("fold", (T, T * N), BF16),
    ("dterm", (HALVES, 2, CHIPS, 16, H), BF16),
    ("dpair", (HALVES, CHIPS, 16, H), BF16),
    ("dsum", (HALVES, CHIPS, 16, H), BF16),
    ("got_d", (HALVES, CHIPS, 16, H), BF16),
    ("mterm", (2, CHIPS, 16, C), BF16),
    ("mpair", (CHIPS, 16, C), BF16),
    ("msum", (CHIPS, 16, C), BF16),
    ("got_m", (CHIPS, 16, C), BF16),
    ("own", (CTX, 8, 128), F32),
    ("got_own", (CTX, 8, 128), F32),
    ("extra", (CTX, 8, 128), F32),
    ("got_extra", (CTX, 8, 128), F32),
    ("last", (8, 8, 128), F32),
    ("got_last", (CTX, 8, 128), F32),
    ("trail", (T + 8, C), F32),
    ("edge", (8, C), F32),
    ("late", (8, C), F32),
)
INPUTS = (
    ("inner", (T, C), BF16),
    ("gate", (T, C), BF16),
    ("grad", (T, C), BF16),
    ("taps", (TAPS, C), F32),
    ("shift", (1, C), F32),
    ("wsel", (PROJ, C), BF16),
    ("wdelta", (C, RANK), BF16),
    ("bias", (1, C), F32),
    ("dlog", (N, C), F32),
    ("skip", (1, C), F32),
)
OUTPUTS = (
    ("inner_grad", (T, C), BF16),
    ("gate_grad", (T, C), BF16),
    ("sel_main", (16, C), F32),
    ("sel_extra", (8, 128), F32),
    ("delta_grad", (16, C), F32),
    ("params", (CTX, 8, 128), F32),
    ("late_params", (8, 8, 128), F32),
)
SEMS = (
    ("in", (len(INPUTS),)),
    ("halo", (2,)),
    ("part", (2, TEN)),
    ("proj", (2, TEN)),
    ("steps", (2, CTX)),
    ("ends", (2, CTX)),
    ("back", (2, CTX)),
    ("psel", (2, TEN)),
    ("sel", (2, TEN)),
    ("dpair", (HALVES, 2)),
    ("dsum", (HALVES, 2, CHIPS)),
    ("mpair", (2,)),
    ("msum", (2, CHIPS)),
    ("own", (2, CTX)),
    ("params", (2, CTX)),
    ("extra", (2, CTX)),
    ("last", (2, CTX)),
    ("spread", (2, CTX)),
    ("edge", (2,)),
)


class Refs:
    pass


def tile_of(v, r, k):
    return v[8 * r : 8 * r + 8, 128 * k : 128 * k + 128]


def wide_of(v):
    return jnp.concatenate([v] * LT, 1)


def lane_sum(v):
    return functools.reduce(jnp.add, [v[:, 128 * k : 128 * k + 128] for k in range(LT)])


def half_lanes(h):
    return pl.ds(pl.multiple_of(h * H, H), H)


def rows_of(block):
    return pl.ds(pl.multiple_of(block * 16, 16), 16)


def convolve(z, first, rows):
    value = jnp.zeros((rows, C), F32) + z.shift[...]
    for k in range(TAPS):
        value = value + z.taps[k : k + 1, :] * z.pad[pl.ds(first + 16 - TAPS + 1 + k, rows), :]
    z.pre[pl.ds(first, rows), :] = value
    s = sigmoid(value)
    conv = value * s
    z.conv[pl.ds(first, rows), :] = conv
    z.half[pl.ds(first, rows), :] = conv.astype(BF16)
    z.slope[pl.ds(first, rows), :] = s * (1.0 + value * (1.0 - s))


def project(z, first, rows):
    half = z.half[pl.ds(first, rows), :]
    blocks = pl.ds(first // ROWS, rows // ROWS)
    shape = (rows // ROWS, ROWS)
    z.part[blocks, :, :RANK] = dot_nt(half, z.wsel[:RANK, :]).astype(BF16).reshape(*shape, RANK)
    z.part[blocks, :, RANK:] = split_tile(dot_nt(half, z.wtail[...])).reshape(*shape, 128)


def border_at(direction, r, k, h):
    return (direction * 8 + r * LT + k) * 2 + h


def summarize(z, h):
    lanes = slice(h * H, h * H + H)
    rate = jnp.exp(z.dlog[:, lanes]) * (-LOG2E)

    def steps(block, carried):
        state, decay, flow = carried
        for i in range(8):
            t = block * 8 + i
            row = pl.ds(t, 1)
            d = jnp.exp2(z.deltas[row, lanes] * rate)
            state = d * state + z.dx[row, lanes] * wide_of(z.bspread[t])
            decay = decay * d
            flow = flow + decay * (z.ocot[row, lanes] * wide_of(z.cspread[t]))
        return state, decay, flow

    zero = jnp.zeros((N, H), F32)
    state, _, flow = lax.fori_loop(0, T // 8, steps, (zero, zero + 1.0, zero))
    for r in range(N // 8):
        for k in range(LT):
            z.ends[border_at(0, r, k, h)] = tile_of(state, r, k)
            z.ends[border_at(1, r, k, h)] = tile_of(flow, r, k)


def edges(z, direction, h):
    return jnp.concatenate(
        [
            jnp.concatenate([z.borders[border_at(direction, r, k, h)] for k in range(LT)], 1)
            for r in range(N // 8)
        ],
        0,
    )


def ones_block():
    return (iota((16, 16 * N), 0) == iota((16, 16 * N), 1) // N).astype(BF16)


def go_forward(z, h):
    lanes = slice(h * H, h * H + H)
    rate2 = jnp.exp(z.dlog[:, lanes]) * (-LOG2E)
    works = (z.work0, z.work1)
    z.work1[...] = jnp.zeros((16 * N, H), BF16)

    def reduce(block, work):
        z.y[rows_of(block + 1), lanes] = dot_nn(z.cblock[rows_of(jnp.maximum(block, 0)), :], work[...])

    def pair(index, state):
        for p in range(2):
            block = index * 2 + p
            reduce(block - 1, works[1 - p])
            for i in range(16):
                t = block * 16 + i
                row = pl.ds(t, 1)
                z.before[t] = state
                d = jnp.exp2(z.deltas[row, lanes] * rate2)
                state = d * state + z.dx[row, lanes] * wide_of(z.bspread[t])
                works[p][N * i : N * i + N, :] = state.astype(BF16)
                z.osum[h, t] = lane_sum(state * z.ocot[row, lanes])
        return state

    lax.fori_loop(0, T // 32, pair, edges(z, 0, h))
    reduce(T // 16 - 1, z.work1)


def go_backward(z, h):
    lanes = slice(h * H, h * H + H)
    rate = -jnp.exp(z.dlog[:, lanes])
    rate2 = rate * LOG2E
    ones = ones_block()
    works, rates = (z.work0, z.work1), (z.rates0, z.rates1)
    z.work0[...] = jnp.zeros((16 * N, H), BF16)
    z.rates0[...] = jnp.zeros((16 * N, H), BF16)

    def reduce(block, work, rated):
        rows = rows_of(block)
        z.along[rows, lanes] = dot_nn(z.bblock[rows_of(jnp.minimum(block, T // 16 - 1)), :], work[...])
        z.wsum[rows, lanes] = dot_nn(ones, rated[...])

    def pair(index, carried):
        flow, total = carried
        for p in reversed(range(2)):
            block = T // 16 - 2 - index * 2 + p
            reduce(block + 1, works[1 - p], rates[1 - p])
            for i in reversed(range(16)):
                t = block * 16 + i
                row = pl.ds(t, 1)
                delta = z.deltas[row, lanes]
                adjoint = z.ocot[row, lanes] * wide_of(z.cspread[t]) + flow
                z.isum[h, t] = lane_sum(adjoint * z.dx[row, lanes])
                works[p][N * i : N * i + N, :] = adjoint.astype(BF16)
                flow = jnp.exp2(delta * rate2) * adjoint
                weighted = flow * z.before[t]
                total = total + weighted * delta
                rates[p][N * i : N * i + N, :] = (weighted * rate).astype(BF16)
        return flow, total

    _, total = lax.fori_loop(0, T // 32, pair, (edges(z, 1, h), jnp.zeros((N, H), F32)))
    reduce(0, z.work0, z.rates0)
    z.decay_part[:, lanes] = total * rate


def gather_sums(z):
    unit = jnp.ones((128, 128), BF16)
    place = iota((T * N, 128), 1) - iota((T * N, 128), 0) % N

    def summed(parts):
        return dot_nn((parts[0] + parts[1]).reshape(T * N, 128).astype(BF16), unit)

    both = jnp.where(
        place == 0, summed(z.isum), jnp.where(place == N, summed(z.osum), 0.0)
    ).astype(BF16)
    z.psel[:, :, RANK:] = dot_nn(z.fold[...], both).astype(BF16).reshape(TEN, ROWS, 128)


def to_sibling(src, dst, sems):
    me = lax.axis_index("context")
    return pltpu.make_async_remote_copy(
        src_ref=src, dst_ref=dst, send_sem=sems.at[0], recv_sem=sems.at[1],
        device_id={"context": me + 1 - 2 * lax.rem(me, 2)}, device_id_type=MESH,
    )


def send_deltas(z, sem, h, pair):
    chip, core = lax.axis_index("context") // 2, lax.rem(lax.axis_index("context"), 2)
    pair.wait()
    z.dsum[h] = (z.dterm[h, core].astype(F32) + z.dpair[h].astype(F32)).astype(BF16)
    sent = Exchange(
        z.dsum.at[h], z.got_d.at[h], sem.dsum.at[h], "chips"
    )
    sent.start()
    z.got_d[h, chip] = z.dsum[h, chip]
    return sent


def layer_kernel(*refs):
    z, given, sem = Refs(), Refs(), Refs()
    refs = list(refs)
    for name, _, _ in INPUTS:
        setattr(given, name, refs.pop(0))
    for name, _, _ in OUTPUTS + INPUTS + SCRATCH:
        setattr(z, name, refs.pop(0))
    for name, _ in SEMS:
        setattr(sem, name, refs.pop(0))
    ctx, ten = lax.axis_index("context"), lax.axis_index("tensor")
    chip, core = ctx // 2, lax.rem(ctx, 2)

    loads = {}
    for i, (name, _, _) in enumerate(INPUTS):
        loads[name] = pltpu.make_async_copy(
            getattr(given, name), getattr(z, name), getattr(sem, "in").at[i]
        )

    for name in ("inner", "taps", "shift", "wsel", "gate", "grad", "dlog", "wdelta", "bias", "skip"):
        loads[name].start()
    greet("tensor", TEN)
    greet("context", CTX)

    for name in ("inner", "taps", "shift"):
        loads[name].wait()
    z.pad[16:, :] = z.inner[...].astype(F32)
    convolve(z, 16, T - 16)
    pl.semaphore_wait(pltpu.get_barrier_semaphore(), TEN - 1 + CTX - 1)
    halo = to_neighbour(z.inner.at[pl.ds(T - 16, 16)], z.halo, sem.halo.at[0], sem.halo.at[1], 1)
    halo.start()
    loads["wsel"].wait()
    tail = z.wsel[RANK:PROJ, :]
    z.wtail[0:32, :] = tail
    z.wtail[32:64, :] = jnp.zeros((32, C), BF16)
    z.wtail[64:96, :] = tail
    z.wtail[96:128, :] = jnp.zeros((32, C), BF16)
    project(z, 16, T - 16)
    halo.wait()
    z.pad[0:16, :] = z.halo[...].astype(F32) * (ctx > 0).astype(F32)
    convolve(z, 0, 16)
    project(z, 0, 16)
    scatter = Exchange(z.part, z.got_part, sem.part, "tensor")
    scatter.start()
    z.got_part[ten] = z.part[ten]

    loads["gate"].wait()
    loads["grad"].wait()
    g = z.gate[...].astype(F32)
    s = sigmoid(g)
    grad = z.grad[...].astype(F32)
    z.ocot[...] = grad * (g * s)
    z.gslope[...] = grad * (s * (1.0 + g * (1.0 - s)))

    scatter.wait_recv()
    total = jnp.sum(z.got_part[...].astype(F32), axis=0)
    bc = total[:, RANK:]
    bc = bc + pltpu.roll(bc, 64, 1)
    z.proj[ten, :, :RANK] = total[:, :RANK].astype(BF16)
    z.proj[ten, :, RANK:] = split_tile(bc)
    gather = Exchange(
        z.proj, z.proj, sem.proj, "tensor", same=True
    )
    gather.start()
    target = iota((WIDE, WIDE), 0)
    source = iota((WIDE, WIDE), 1)
    place = target % 256
    order = jnp.where(
        target < RANK,
        (place // 16 * 2 + target // 256) * 17 + place % 16,
        (target - RANK) * 17 + 16,
    )
    z.order[...] = ((order == source) & (target < PROJ)).astype(BF16)
    z.fold[...] = (iota((T, T * N), 0) == iota((T, T * N), 1) // N).astype(BF16)
    for name in ("dlog", "wdelta", "bias", "skip"):
        loads[name].wait()
    gather.wait_recv()

    flat = z.proj[...].reshape(T, WIDE)
    raw = dot_nt(flat[:, :RANK], z.wdelta[...]) + z.bias[...]
    step = jnp.maximum(raw, 0.0) + jnp.log1p(jnp.exp(-jnp.abs(raw)))
    z.deltas[...] = step
    lengths = jnp.sum(step, axis=0, keepdims=True)
    for k in range(8):
        z.steps[ctx, k : k + 1, :] = lengths[:, 128 * k : 128 * k + 128]
    steps = Exchange(
        z.steps, z.steps, sem.steps, "context", same=True
    )
    steps.start()
    z.sig[...] = sigmoid(raw)
    z.dx[...] = step * z.conv[...]
    spread(z, flat[:, RANK:])
    ends = Exchange(z.ends, z.got_ends, sem.ends, "context")
    for h in range(HALVES):
        summarize(z, h)
        ends.to_core(h, lambda copy: copy.start())

    z.got_ends[ctx] = z.ends[ctx]
    backward = chip // 8
    at_row = pl.ds(pl.multiple_of(lax.rem(chip, 8) // LT * 8, 8), 8)
    at_lane = core * LT + lax.rem(chip, LT)
    rate = jnp.exp(z.dlog[at_row, pl.ds(pl.multiple_of(at_lane * 128, 128), 128)]) * (-LOG2E)
    steps.wait_recv()

    def shrink(i, _):
        z.decays[i] = jnp.exp2(rate * z.steps[i, pl.ds(at_lane, 1), :])
        return 0

    lax.fori_loop(0, CTX, shrink, 0)
    column = iota((128, 16 * N), 1)
    same = iota((T, 16 * N), 0) % 16 == column // N
    lane = iota((128, 16 * N), 0) % 64
    z.bblock[...] = jnp.where(
        same, dot_nn(flat[:, RANK:], (lane == column % N).astype(BF16)), 0.0
    ).astype(BF16)
    z.cblock[...] = jnp.where(
        same, dot_nn(flat[:, RANK:], (lane == column % N + N).astype(BF16)), 0.0
    ).astype(BF16)
    ends.wait_recv()

    def follow(i, carried):
        at = i + backward * (CTX - 1 - 2 * i)
        z.back[at] = carried
        return z.decays[at] * carried + z.got_ends[at]

    lax.fori_loop(0, CTX, follow, jnp.zeros((8, 128), F32))
    home = Exchange(z.back, z.borders, sem.back, "context")
    home.start()
    z.borders[ctx] = z.back[ctx]
    scatter.wait_send()
    gather.wait_send()
    steps.wait_send()

    rank_part = jnp.zeros((T, RANK), F32)
    dpairs, deltas, sides = [], [], []
    for h in range(HALVES):
        lanes = slice(h * H, h * H + H)
        home.to_core(h, lambda copy: copy.wait_recv())
        go_forward(z, h)
        if h > 0:
            deltas.append(send_deltas(z, sem, h - 1, dpairs[h - 1]))
        go_backward(z, h)
        near = z.along[0:T, lanes]
        raw_cot = (z.wsum[0:T, lanes] + z.conv[:, lanes] * near) * z.sig[:, lanes]
        raw_half = raw_cot.astype(BF16)
        rank_part = rank_part + dot_nn(raw_half, z.wdelta[lanes, :])
        if h == HALVES - 1:
            gather_sums(z)
            z.psel[:, :, :RANK] = rank_part.astype(BF16).reshape(TEN, ROWS, RANK)
            scatter2 = Exchange(z.psel, z.got_psel, sem.psel, "tensor")
            scatter2.start()
            z.got_psel[ten] = z.psel[ten]
        term = dot_tn(flat[:, :RANK], raw_half).astype(BF16).reshape(CHIPS, 2, 16, H)
        z.dterm[h, 0] = term[:, 0]
        z.dterm[h, 1] = term[:, 1]
        dpairs.append(to_sibling(z.dterm.at[h, 1 - core], z.dpair.at[h], sem.dpair.at[h]))
        dpairs[h].start()
        cot, gain, conv = z.ocot[:, lanes], z.skip[:, lanes], z.conv[:, lanes]
        z.gate_grad[:, lanes] = (
            z.gslope[:, lanes] * (z.y[16 : T + 16, lanes] + gain * conv)
        ).astype(BF16)
        z.direct[:, lanes] = gain * cot + z.deltas[:, lanes] * near
        sides.append(
            jnp.concatenate(
                [
                    jnp.sum(raw_cot, axis=0, keepdims=True),
                    jnp.sum(cot * conv, axis=0, keepdims=True),
                    jnp.zeros((6, H), F32),
                ],
                0,
            )
        )

    scatter2.wait_recv()
    z.sel[ten] = jnp.sum(z.got_psel[...].astype(F32), axis=0).astype(BF16)
    gather2 = Exchange(z.sel, z.sel, sem.sel, "tensor", same=True)
    gather2.start()
    deltas.append(send_deltas(z, sem, HALVES - 1, dpairs[HALVES - 1]))
    early = jnp.concatenate(sides, 1)
    for k in range(8):
        lanes = slice(128 * k, 128 * k + 128)
        z.own[k] = z.decay_part[0:8, lanes]
        z.own[8 + k] = z.decay_part[8:16, lanes]
        z.own[16 + k] = early[:, lanes]
        z.own[24 + k] = jnp.zeros((8, 128), F32)
    sums = Exchange(z.own, z.got_own, sem.own, "context")
    sums.start()
    z.got_own[ctx] = z.own[ctx]
    gather2.wait_recv()
    select_cot = z.sel[...].reshape(T, WIDE)

    turned = dot_nt(z.order[...], select_cot).astype(BF16)
    z.mterm[...] = dot_nn(turned[:RANK, :], z.half[...]).astype(BF16).reshape(2, CHIPS, 16, C)
    mpair = to_sibling(z.mterm.at[1 - core], z.mpair, sem.mpair)
    mpair.start()
    pre_cot = (z.direct[...] + dot_nn(select_cot[:, :PROJ], z.wsel[...])) * z.slope[...]
    z.trail[0:T, :] = pre_cot
    z.edge[...] = pre_cot[0:8, :]
    below = to_neighbour(z.edge, z.late, sem.edge.at[0], sem.edge.at[1], -1)
    below.start()
    rows = [jnp.sum(pre_cot, axis=0, keepdims=True)]
    for k in range(TAPS):
        rows.append(
            jnp.sum(pre_cot * z.pad[pl.ds(16 - TAPS + 1 + k, T), :], axis=0, keepdims=True)
        )
    rows = jnp.concatenate(rows + [jnp.zeros((3, C), F32)], 0)
    for k in range(8):
        z.last[k] = rows[:, 128 * k : 128 * k + 128]
    lasts = ToEighth(z.last, z.got_last, sem.last)
    lasts.start()
    z.got_last[ctx] = z.last[ctx // 4]
    mpair.wait()
    z.msum[...] = (z.mterm[core].astype(F32) + z.mpair[...].astype(F32)).astype(BF16)
    mains = Exchange(
        z.msum, z.got_m, sem.msum, "chips"
    )
    mains.start()
    z.got_m[chip] = z.msum[chip]
    sums.wait_recv()
    z.params[ctx] = jnp.sum(z.got_own[...], axis=0)
    spreads = Exchange(
        z.params, z.params, sem.params, "context", same=True
    )
    spreads.start()
    extra = dot_nn(turned[RANK : RANK + CTX, :], z.half[...])
    for k in range(8):
        z.extra[:, k, :] = extra[:, 128 * k : 128 * k + 128]
    extras = Exchange(z.extra, z.got_extra, sem.extra, "context")
    extras.start()
    z.got_extra[ctx] = z.extra[ctx]

    below.wait()
    z.trail[T:, :] = z.late[...] * (ctx < CTX - 1).astype(F32)
    result = jnp.zeros((T, C), F32)
    for k in range(TAPS):
        result = result + z.taps[k : k + 1, :] * z.trail[pl.ds(TAPS - 1 - k, T), :]
    z.inner_grad[...] = result.astype(BF16)

    lasts.wait_recv()

    @pl.when(lax.rem(ctx, 4) == 0)
    def _():
        z.late_params[ctx // 4] = jnp.sum(z.got_last[...], axis=0)

    shares = ToEighth(
        z.late_params, z.late_params, sem.spread, back=True
    )
    shares.start()
    for h in range(HALVES):
        deltas[h].wait_recv()
        z.delta_grad[:, h * H : h * H + H] = jnp.sum(z.got_d[h].astype(F32), axis=0)
    for exchange in (ends, home, scatter2, gather2, sums, deltas[0], deltas[1]):
        exchange.wait_send()
    extras.wait_recv()
    z.sel_extra[...] = jnp.sum(z.got_extra[...], axis=0)
    mains.wait_recv()
    z.sel_main[...] = jnp.sum(z.got_m[...].astype(F32), axis=0)
    spreads.wait_recv()
    shares.wait_recv()
    for exchange in (lasts, mains, spreads, extras, shares):
        exchange.wait_send()


def layer(*args):
    return pl.pallas_call(
        layer_kernel,
        out_shape=[jax.ShapeDtypeStruct(shape, kind) for _, shape, kind in OUTPUTS],
        in_specs=[pl.BlockSpec(memory_space=pl.ANY)] * len(INPUTS),
        out_specs=[VMEM] * len(OUTPUTS),
        scratch_shapes=[pltpu.VMEM(shape, kind) for _, shape, kind in INPUTS + SCRATCH]
        + [pltpu.SemaphoreType.DMA(shape) for _, shape in SEMS],
        compiler_params=pltpu.CompilerParams(
            collective_id=0, has_side_effects=True, vmem_limit_bytes=56 << 20
        ),
        name="layer",
    )(*args)


def finish_kernel(
    inner_grad, gate_grad, sel_main, sel_extra, delta, params, late,
    inner_out, gate_out, taps_out, shift_out, sel_out, delta_out, bias_out, decay_out, skip_out,
):
    inner_out[...] = inner_grad[...]
    gate_out[...] = gate_grad[...]
    sel_out[0:16, :] = sel_main[...]
    delta_out[...] = delta[...]
    for k in range(8):
        lanes = slice(128 * k, 128 * k + 128)
        sel_out[16:17, lanes] = sel_extra[k : k + 1, :]
        decay_out[0:8, lanes] = params[k]
        decay_out[8:16, lanes] = params[8 + k]
        rows = params[16 + k]
        bias_out[:, lanes] = rows[0:1, :]
        skip_out[:, lanes] = rows[1:2, :]
        shift_out[:, lanes] = late[k, 0:1, :]
        taps_out[:, lanes] = late[k, 1:5, :]


def finish(*args):
    shapes = ((T, C), (T, C), (TAPS, C), (1, C), (17, C), (16, C), (1, C), (N, C), (1, C))
    return pl.pallas_call(
        finish_kernel,
        out_shape=[
            jax.ShapeDtypeStruct(shape, BF16 if i < 2 else F32) for i, shape in enumerate(shapes)
        ],
        in_specs=[VMEM] * 7,
        out_specs=[VMEM] * 9,
        name="finish",
    )(*args)


def body(
    inner_in, gate_in, out_grad, kernel, kernel_shift, select_proj, delta_proj, delta_bias,
    decay_log, skip_gain,
):
    parts = layer(
        inner_in, gate_in, out_grad, kernel.T, kernel_shift[None], select_proj, delta_proj,
        delta_bias[None], decay_log.T, skip_gain[None],
    )
    inner_grad, gate_grad, taps, shift, select, delta, bias, decay, skip = finish(*parts)
    return (
        inner_grad, gate_grad, taps.T, shift[0], select, delta.T, bias[0], decay.T, skip[0],
    )


def solution(mesh):
    return jax.shard_map(
        body,
        mesh=mesh,
        in_specs=(
            P("context", "tensor"),
            P("context", "tensor"),
            P("context", "tensor"),
            P("tensor", None),
            P("tensor"),
            P(None, "tensor"),
            P("tensor", None),
            P("tensor"),
            P("tensor", None),
            P("tensor"),
        ),
        out_specs=(
            P("context", "tensor"),
            P("context", "tensor"),
            P("tensor", None),
            P("tensor"),
            P("context", "tensor"),
            P("tensor", "context"),
            P("tensor"),
            P("tensor", None),
            P("tensor"),
        ),
        check_vma=False,
    )
```

```python
import functools

import jax
import jax.numpy as jnp
from jax import lax
from jax.experimental import pallas as pl
from jax.experimental.pallas import tpu as pltpu
from jax.sharding import PartitionSpec as P

N = 16
RANK = 512
TAPS = 4
PROJ = 544
WIDE = 640
T = 128
C = 1024
H = 512
CTX = 32
TEN = 8
CHIPS = CTX // 2
ROWS = T // TEN
LOG2E = 1.4426950408889634
MESH = pl.DeviceIdType.MESH
F32 = jnp.float32
BF16 = jnp.bfloat16
VMEM = pl.BlockSpec(memory_space=pltpu.VMEM)


def dot_nn(a, b):
    return lax.dot_general(a, b, (((1,), (0,)), ((), ())), preferred_element_type=F32)


def dot_nt(a, b):
    return lax.dot_general(a, b, (((1,), (1,)), ((), ())), preferred_element_type=F32)


def dot_tn(a, b):
    return lax.dot_general(a, b, (((0,), (0,)), ((), ())), preferred_element_type=F32)


def iota(shape, axis):
    return lax.broadcasted_iota(jnp.int32, shape, axis)


def sigmoid(v):
    return jax.nn.sigmoid(v)


def silu_slope(v):
    s = sigmoid(v)
    return s * (1.0 + v * (1.0 - s))


def split_tile(v):
    high = v.astype(BF16).astype(F32)
    return jnp.where(iota(v.shape, 1) < 64, high, v - high).astype(BF16)


def far_first(k, size):
    if isinstance(k, int):
        return size // 2 + (k + 1) // 2 * (1 - 2 * (k % 2))
    return size // 2 + (k + 1) // 2 * (1 - 2 * lax.rem(k, 2))


def peer_of(group, k):
    if group == "tensor":
        at = lax.axis_index("tensor")
        peer = lax.rem(at + far_first(k, TEN), TEN)
        return at, peer, {"tensor": peer}
    me = lax.axis_index("context")
    place, core = (k // 2, 1 - k % 2) if group == "context" else (k, 0)
    x = lax.rem(me // 8 + far_first(place // 4, 4), 4)
    y = lax.rem(me // 2 + far_first(place % 4, 4), 4)
    peer = (x * 4 + y) * 2 + lax.rem(me + core, 2)
    if group == "chips":
        return me // 2, x * 4 + y, {"context": peer}
    return me, peer, {"context": peer}


PEERS = {"tensor": TEN - 1, "context": CTX - 1, "chips": CHIPS - 1}


class Exchange:
    def __init__(self, src, dst, sems, group, same=False):
        self.src, self.dst, self.send, self.recv = src, dst, sems.at[0], sems.at[1]
        self.group, self.same = group, same

    def copy(self, k):
        at, peer, target = peer_of(self.group, k)
        return pltpu.make_async_remote_copy(
            src_ref=self.src.at[at] if self.same else self.src.at[peer],
            dst_ref=self.dst.at[at],
            send_sem=self.send.at[k],
            recv_sem=self.recv.at[k],
            device_id=target,
            device_id_type=MESH,
        )

    def every(self, act):
        lax.fori_loop(0, PEERS[self.group], lambda k, _: (act(self.copy(k)), 0)[1], 0)

    def start(self):
        for k in range(PEERS[self.group]):
            self.copy(k).start()

    def wait_recv(self):
        self.every(lambda copy: copy.wait_recv())

    def wait_send(self):
        self.every(lambda copy: copy.wait_send())

    def to_core(self, core, act):
        other = lax.rem(lax.axis_index("context") + core, 2)
        lax.fori_loop(
            0, CHIPS - 1 + other, lambda q, _: (act(self.copy(2 * q + 1 - other)), 0)[1], 0
        )


def greet(group):
    barrier = pltpu.get_barrier_semaphore()

    for k in range(PEERS[group]):
        pl.semaphore_signal(barrier, inc=1, device_id=peer_of(group, k)[2], device_id_type=MESH)


def to_neighbour(src, dst, send, recv, step):
    peer = lax.rem(lax.axis_index("context") + step + CTX, CTX)
    return pltpu.make_async_remote_copy(
        src_ref=src, dst_ref=dst, send_sem=send, recv_sem=recv,
        device_id={"context": peer}, device_id_type=MESH,
    )


def spread(z, tile):
    rows = T * N
    repeat = (iota((rows, T), 0) // N == iota((rows, T), 1)).astype(BF16)
    each = dot_nn(repeat, tile)
    place = iota((rows, 128), 1) % 64 - iota((rows, 128), 0) % N
    unit = jnp.ones((128, 128), BF16)
    z.bspread[...] = dot_nn(jnp.where(place == 0, each, 0.0).astype(BF16), unit).reshape(T, N, 128)
    z.cspread[...] = dot_nn(jnp.where(place == N, each, 0.0).astype(BF16), unit).reshape(T, N, 128)


HALVES = C // H
LT = H // 128

SCRATCH = (
    ("pad", (T + 16, C), F32),
    ("pre", (T, C), F32),
    ("conv", (T, C), F32),
    ("slope", (T, C), F32),
    ("half", (T, C), BF16),
    ("ocot", (T, C), F32),
    ("gslope", (T, C), F32),
    ("sig", (T, C), F32),
    ("deltas", (T, C), F32),
    ("dx", (T, C), F32),
    ("y", (T, C), F32),
    ("along", (T, C), F32),
    ("wsum", (T, C), F32),
    ("direct", (T, C), F32),
    ("halo", (16, C), BF16),
    ("wtail", (128, C), BF16),
    ("part", (TEN, ROWS, WIDE), BF16),
    ("got_part", (TEN, ROWS, WIDE), BF16),
    ("proj", (TEN, ROWS, WIDE), BF16),
    ("bspread", (T, N, 128), F32),
    ("cspread", (T, N, 128), F32),
    ("ends", (CTX, 9, 128), F32),
    ("got_ends", (CTX, 9, 128), F32),
    ("decays", (CTX, 8, 128), F32),
    ("back", (CTX, 8, 128), F32),
    ("borders", (CTX, 8, 128), F32),
    ("before", (T, N, H), F32),
    ("isum", (HALVES, T, N, 128), F32),
    ("osum", (HALVES, T, N, 128), F32),
    ("decay_part", (N, C), F32),
    ("psel", (TEN, ROWS, WIDE), BF16),
    ("got_psel", (TEN, ROWS, WIDE), BF16),
    ("sel", (TEN, ROWS, WIDE), BF16),
    ("order", (WIDE, WIDE), BF16),
    ("fold", (T, T * N), BF16),
    ("dterm", (HALVES, 2, CHIPS, 16, H), BF16),
    ("dpair", (HALVES, CHIPS, 16, H), BF16),
    ("dsum", (HALVES, CHIPS, 16, H), BF16),
    ("got_d", (HALVES, CHIPS, 16, H), BF16),
    ("mterm", (2, CHIPS, 16, C), BF16),
    ("mpair", (CHIPS, 16, C), BF16),
    ("msum", (CHIPS, 16, C), BF16),
    ("got_m", (CHIPS, 16, C), BF16),
    ("own", (2, CHIPS, 2, 8, 128), F32),
    ("opair", (CHIPS, 2, 8, 128), F32),
    ("ojoin", (CHIPS, 2, 8, 128), F32),
    ("got_own", (CHIPS, 2, 8, 128), F32),
    ("params", (2, CHIPS, 8, 128), F32),
    ("wdperm", (C, WIDE), BF16),
    ("wsperm", (WIDE, C), BF16),
    ("trail", (T + 8, C), F32),
    ("edge", (8, C), F32),
    ("late", (8, C), F32),
)
INPUTS = (
    ("inner", (T, C), BF16),
    ("gate", (T, C), BF16),
    ("grad", (T, C), BF16),
    ("taps", (TAPS, C), F32),
    ("shift", (1, C), F32),
    ("wsel", (PROJ, C), BF16),
    ("wdelta", (C, RANK), BF16),
    ("bias", (1, C), F32),
    ("dlog", (N, C), F32),
    ("skip", (1, C), F32),
)
OUTPUTS = (
    ("inner_grad", (T, C), BF16),
    ("gate_grad", (T, C), BF16),
    ("taps_grad", (TAPS, C), F32),
    ("shift_grad", (1, C), F32),
    ("select_grad", (17, C), F32),
    ("delta_grad", (16, C), F32),
    ("bias_grad", (1, C), F32),
    ("decay_grad", (N, C), F32),
    ("skip_grad", (1, C), F32),
)
SEMS = (
    ("in", (len(INPUTS),)),
    ("halo", (2,)),
    ("part", (2, TEN)),
    ("proj", (2, TEN)),
    ("ends", (2, CTX)),
    ("back", (2, CTX)),
    ("psel", (2, TEN)),
    ("sel", (2, TEN)),
    ("dpair", (HALVES, 2)),
    ("dsum", (HALVES, 2, CHIPS)),
    ("mpair", (2,)),
    ("msum", (2, CHIPS)),
    ("opair", (2,)),
    ("own", (2, CHIPS)),
    ("params", (2, CHIPS)),
    ("ppair", (2,)),
    ("edge", (2,)),
)


class Refs:
    pass


def tile_of(v, r, k):
    return v[8 * r : 8 * r + 8, 128 * k : 128 * k + 128]


def wide_of(v):
    return jnp.concatenate([v] * LT, 1)


def lane_sum(v):
    return functools.reduce(jnp.add, [v[:, 128 * k : 128 * k + 128] for k in range(LT)])


def half_lanes(h):
    return pl.ds(pl.multiple_of(h * H, H), H)


def convolve(z, first, rows):
    value = jnp.zeros((rows, C), F32) + z.shift[...]
    for k in range(TAPS):
        value = value + z.taps[k : k + 1, :] * z.pad[pl.ds(first + 16 - TAPS + 1 + k, rows), :]
    z.pre[pl.ds(first, rows), :] = value
    s = sigmoid(value)
    conv = value * s
    z.conv[pl.ds(first, rows), :] = conv
    z.half[pl.ds(first, rows), :] = conv.astype(BF16)
    z.slope[pl.ds(first, rows), :] = s * (1.0 + value * (1.0 - s))


def project(z, first, rows):
    half = z.half[pl.ds(first, rows), :]
    blocks = pl.ds(first // ROWS, rows // ROWS)
    shape = (rows // ROWS, ROWS)
    z.part[blocks, :, :RANK] = dot_nt(half, z.wsel[:RANK, :]).astype(BF16).reshape(*shape, RANK)
    z.part[blocks, :, RANK:] = split_tile(dot_nt(half, z.wtail[...])).reshape(*shape, 128)


def border_at(direction, r, k, h):
    return (direction * 8 + r * LT + k) * 2 + h


def summarize(z, h, lengths):
    lanes = slice(h * H, h * H + H)
    rate = jnp.exp(z.dlog[:, lanes]) * (-LOG2E)

    def steps(block, carried):
        state, decay, flow = carried
        for i in range(8):
            t = block * 8 + i
            row = pl.ds(t, 1)
            d = jnp.exp2(z.deltas[row, lanes] * rate)
            state = d * state + z.dx[row, lanes] * wide_of(z.bspread[t])
            decay = decay * d
            flow = flow + decay * (z.ocot[row, lanes] * wide_of(z.cspread[t]))
        return state, decay, flow

    zero = jnp.zeros((N, H), F32)
    state, _, flow = lax.fori_loop(0, T // 8, steps, (zero, zero + 1.0, zero))
    for r in range(N // 8):
        for k in range(LT):
            for direction, value in enumerate((state, flow)):
                at = border_at(direction, r, k, h)
                z.ends[at, 0:8, :] = tile_of(value, r, k)
                z.ends[at, 8:9, :] = lengths[:, h * H + 128 * k : h * H + 128 * k + 128]


def edges(z, direction, h):
    return jnp.concatenate(
        [
            jnp.concatenate([z.borders[border_at(direction, r, k, h)] for k in range(LT)], 1)
            for r in range(N // 8)
        ],
        0,
    )


class Fold:
    def __init__(self, rising):
        self.rising, self.waiting = rising, {}

    def push(self, value):
        value, step = value[0:8, :] + value[8:16, :], 1
        sub = iota(value.shape, 0)
        while step in self.waiting:
            other = self.waiting.pop(step)
            a, b = (other, value) if self.rising else (value, other)
            low = sub // step % 2 == 0
            value = jnp.where(low, a, b) + pltpu.roll(jnp.where(low, b, a), step, 0)
            step *= 2
        self.waiting[step] = value

    def result(self):
        return self.waiting[8]


def rows_of8(block):
    return pl.ds(pl.multiple_of(block * 8, 8), 8)


def go_forward(z, h):
    lanes = slice(h * H, h * H + H)
    rate2 = jnp.exp(z.dlog[:, lanes]) * (-LOG2E)

    def forward(block, state):
        y = Fold(True)
        for i in range(8):
            t = block * 8 + i
            row = pl.ds(t, 1)
            z.before[t] = state
            d = jnp.exp2(z.deltas[row, lanes] * rate2)
            state = d * state + z.dx[row, lanes] * wide_of(z.bspread[t])
            y.push(state * wide_of(z.cspread[t]))
            z.osum[h, t] = lane_sum(state * z.ocot[row, lanes])
        z.y[rows_of8(block), lanes] = y.result()
        return state

    lax.fori_loop(0, T // 8, forward, edges(z, 0, h))


def go_backward(z, h):
    lanes = slice(h * H, h * H + H)
    rate2 = jnp.exp(z.dlog[:, lanes]) * (-LOG2E)

    def backward(index, carried):
        flow, total = carried
        block = T // 8 - 1 - index
        along, wsum = Fold(False), Fold(False)
        for i in reversed(range(8)):
            t = block * 8 + i
            row = pl.ds(t, 1)
            delta = z.deltas[row, lanes]
            adjoint = z.ocot[row, lanes] * wide_of(z.cspread[t]) + flow
            z.isum[h, t] = lane_sum(adjoint * z.dx[row, lanes])
            along.push(adjoint * wide_of(z.bspread[t]))
            flow = jnp.exp2(delta * rate2) * adjoint
            weighted = flow * z.before[t]
            total = total + weighted * delta
            wsum.push(weighted * rate2)
        z.along[rows_of8(block), lanes] = along.result()
        z.wsum[rows_of8(block), lanes] = wsum.result() * (1.0 / LOG2E)
        return flow, total

    _, total = lax.fori_loop(0, T // 8, backward, (edges(z, 1, h), jnp.zeros((N, H), F32)))
    z.decay_part[:, lanes] = total * (rate2 * (1.0 / LOG2E))


def gather_sums(z):
    unit = jnp.ones((128, 128), BF16)
    place = iota((T * N, 128), 1) - iota((T * N, 128), 0) % N

    def summed(parts):
        return dot_nn((parts[0] + parts[1]).reshape(T * N, 128).astype(BF16), unit)

    both = jnp.where(
        place == 0, summed(z.isum), jnp.where(place == N, summed(z.osum), 0.0)
    ).astype(BF16)
    return dot_nn(z.fold[...], both)


def to_sibling(src, dst, sems):
    me = lax.axis_index("context")
    return pltpu.make_async_remote_copy(
        src_ref=src, dst_ref=dst, send_sem=sems.at[0], recv_sem=sems.at[1],
        device_id={"context": me + 1 - 2 * lax.rem(me, 2)}, device_id_type=MESH,
    )


def send_deltas(z, sem, h, pair):
    chip, core = lax.axis_index("context") // 2, lax.rem(lax.axis_index("context"), 2)
    pair.wait()
    z.dsum[h] = (z.dterm[h, core].astype(F32) + z.dpair[h].astype(F32)).astype(BF16)
    sent = Exchange(
        z.dsum.at[h], z.got_d.at[h], sem.dsum.at[h], "chips"
    )
    sent.start()
    z.got_d[h, chip] = z.dsum[h, chip]
    return sent


def layer_kernel(*refs):
    z, given, sem = Refs(), Refs(), Refs()
    refs = list(refs)
    for name, _, _ in INPUTS:
        setattr(given, name, refs.pop(0))
    for name, _, _ in OUTPUTS + INPUTS + SCRATCH:
        setattr(z, name, refs.pop(0))
    for name, _ in SEMS:
        setattr(sem, name, refs.pop(0))
    ctx, ten = lax.axis_index("context"), lax.axis_index("tensor")
    chip, core = ctx // 2, lax.rem(ctx, 2)

    greet("context")
    greet("tensor")
    loads = {}
    for i, (name, _, _) in enumerate(INPUTS):
        loads[name] = pltpu.make_async_copy(
            getattr(given, name), getattr(z, name), getattr(sem, "in").at[i]
        )

    for name in ("inner", "taps", "shift", "wsel", "gate", "grad", "dlog", "wdelta", "bias", "skip"):
        loads[name].start()

    for name in ("inner", "taps", "shift"):
        loads[name].wait()
    z.pad[16:, :] = z.inner[...].astype(F32)
    convolve(z, 16, T - 16)
    pl.semaphore_wait(pltpu.get_barrier_semaphore(), TEN - 1 + CTX - 1)
    halo = to_neighbour(z.inner.at[pl.ds(T - 16, 16)], z.halo, sem.halo.at[0], sem.halo.at[1], 1)
    halo.start()
    loads["wsel"].wait()
    tail = z.wsel[RANK:PROJ, :]
    z.wtail[0:32, :] = tail
    z.wtail[32:64, :] = jnp.zeros((32, C), BF16)
    z.wtail[64:96, :] = tail
    z.wtail[96:128, :] = jnp.zeros((32, C), BF16)
    project(z, 16, T - 16)
    halo.wait()
    z.pad[0:16, :] = z.halo[...].astype(F32) * (ctx > 0).astype(F32)
    convolve(z, 0, 16)
    project(z, 0, 16)
    scatter = Exchange(z.part, z.got_part, sem.part, "tensor")
    scatter.start()
    z.got_part[ten] = z.part[ten]

    loads["gate"].wait()
    loads["grad"].wait()
    g = z.gate[...].astype(F32)
    s = sigmoid(g)
    grad = z.grad[...].astype(F32)
    z.ocot[...] = grad * (g * s)
    z.gslope[...] = grad * (s * (1.0 + g * (1.0 - s)))

    scatter.wait_recv()
    total = jnp.sum(z.got_part[...].astype(F32), axis=0)
    bc = total[:, RANK:]
    bc = bc + pltpu.roll(bc, 64, 1)
    z.proj[ten, :, :RANK] = total[:, :RANK].astype(BF16)
    z.proj[ten, :, RANK:] = split_tile(bc)
    gather = Exchange(
        z.proj, z.proj, sem.proj, "tensor", same=True
    )
    gather.start()
    target = iota((WIDE, WIDE), 0)
    source = iota((WIDE, WIDE), 1)
    place = target % 256
    rest = target - RANK
    order = jnp.where(
        target < RANK,
        (place // 16 * 2 + target // 256) * 17 + place % 16,
        (rest % 16 * 2 + rest // 16) * 17 + 16,
    )
    order = ((order == source) & (target < PROJ)).astype(BF16)
    z.order[...] = order
    loads["wdelta"].wait()
    z.wdperm[...] = dot_nt(z.wdelta[...], order[:, :RANK]).astype(BF16)
    z.wsperm[...] = dot_nn(order[:, :PROJ], z.wsel[...]).astype(BF16)
    z.fold[...] = (iota((T, T * N), 0) == iota((T, T * N), 1) // N).astype(BF16)
    for name in ("dlog", "bias", "skip"):
        loads[name].wait()
    gather.wait_recv()

    flat = z.proj[...].reshape(T, WIDE)
    raw = dot_nt(flat[:, :RANK], z.wdelta[...]) + z.bias[...]
    step = jnp.maximum(raw, 0.0) + jnp.log1p(jnp.exp(-jnp.abs(raw)))
    z.deltas[...] = step
    lengths = jnp.sum(step, axis=0, keepdims=True)
    z.sig[...] = sigmoid(raw)
    z.dx[...] = step * z.conv[...]
    spread(z, flat[:, RANK:])
    ends = Exchange(z.ends, z.got_ends, sem.ends, "context")
    for h in range(HALVES):
        summarize(z, h, lengths)
        ends.to_core(h, lambda copy: copy.start())

    z.got_ends[ctx] = z.ends[ctx]
    backward = chip // 8
    at_row = pl.ds(pl.multiple_of(lax.rem(chip, 8) // LT * 8, 8), 8)
    at_lane = core * LT + lax.rem(chip, LT)
    rate = jnp.exp(z.dlog[at_row, pl.ds(pl.multiple_of(at_lane * 128, 128), 128)]) * (-LOG2E)
    ends.wait_recv()
    z.decays[...] = jnp.exp2(rate[None] * z.got_ends[:, 8:9, :])
    carried = jnp.zeros((8, 128), F32)
    for i in range(CTX):
        at = i + backward * (CTX - 1 - 2 * i)
        z.back[at] = carried
        carried = z.decays[at] * carried + z.got_ends[at, 0:8, :]
    home = Exchange(z.back, z.borders, sem.back, "context")
    home.start()
    z.borders[ctx] = z.back[ctx]
    scatter.wait_send()
    gather.wait_send()

    select_part = jnp.zeros((T, WIDE), F32)
    dpairs, deltas, sides = [], [], []
    for h in range(HALVES):
        lanes = slice(h * H, h * H + H)
        home.to_core(h, lambda copy: copy.wait_recv())
        go_forward(z, h)
        if h > 0:
            deltas.append(send_deltas(z, sem, h - 1, dpairs[h - 1]))
        go_backward(z, h)
        near = z.along[:, lanes]
        raw_cot = (z.wsum[:, lanes] + z.conv[:, lanes] * near) * z.sig[:, lanes]
        raw_half = raw_cot.astype(BF16)
        select_part = select_part + dot_nn(raw_half, z.wdperm[lanes, :])
        if h == HALVES - 1:
            select_part = select_part + dot_nt(gather_sums(z).astype(BF16), z.order[:, RANK:])
            z.psel[...] = select_part.astype(BF16).reshape(TEN, ROWS, WIDE)
            scatter2 = Exchange(z.psel, z.got_psel, sem.psel, "tensor")
            scatter2.start()
            z.got_psel[ten] = z.psel[ten]
        term = dot_tn(flat[:, :RANK], raw_half).astype(BF16).reshape(CHIPS, 2, 16, H)
        z.dterm[h, 0] = term[:, 0]
        z.dterm[h, 1] = term[:, 1]
        dpairs.append(to_sibling(z.dterm.at[h, 1 - core], z.dpair.at[h], sem.dpair.at[h]))
        dpairs[h].start()
        cot, gain, conv = z.ocot[:, lanes], z.skip[:, lanes], z.conv[:, lanes]
        z.gate_grad[:, lanes] = (
            z.gslope[:, lanes] * (z.y[:, lanes] + gain * conv)
        ).astype(BF16)
        z.direct[:, lanes] = gain * cot + z.deltas[:, lanes] * near
        sides.append(
            jnp.concatenate(
                [
                    jnp.sum(raw_cot, axis=0, keepdims=True),
                    jnp.sum(cot * conv, axis=0, keepdims=True),
                ],
                0,
            )
        )

    scatter2.wait_recv()
    z.sel[ten] = jnp.sum(z.got_psel[...].astype(F32), axis=0).astype(BF16)
    gather2 = Exchange(z.sel, z.sel, sem.sel, "tensor", same=True)
    gather2.start()
    deltas.append(send_deltas(z, sem, HALVES - 1, dpairs[HALVES - 1]))
    early = jnp.concatenate(sides, 1)
    for k in range(8):
        lanes = slice(128 * k, 128 * k + 128)
        z.own[0, k, 0] = z.decay_part[0:8, lanes]
        z.own[0, 8 + k, 0] = z.decay_part[8:16, lanes]
        z.own[1, 8 + k, 0] = jnp.zeros((8, 128), F32)
    gather2.wait_recv()
    select_cot = z.sel[...].reshape(T, WIDE)

    pre_cot = (z.direct[...] + dot_nn(select_cot, z.wsperm[...])) * z.slope[...]
    z.trail[0:T, :] = pre_cot
    z.edge[...] = pre_cot[0:8, :]
    below = to_neighbour(z.edge, z.late, sem.edge.at[0], sem.edge.at[1], -1)
    below.start()
    rows = [early, jnp.sum(pre_cot, axis=0, keepdims=True)]
    for k in range(TAPS):
        rows.append(
            jnp.sum(pre_cot * z.pad[pl.ds(16 - TAPS + 1 + k, T), :], axis=0, keepdims=True)
        )
    rows = jnp.concatenate(rows + [jnp.zeros((1, C), F32)], 0)
    extra = dot_tn(select_cot[:, RANK:], z.half[...])
    for k in range(8):
        lanes = slice(128 * k, 128 * k + 128)
        z.own[1, k, 0] = rows[:, lanes]
        z.own[0, :, 1, k, :] = extra[0:CHIPS, lanes]
        z.own[1, :, 1, k, :] = extra[CHIPS:CTX, lanes]
    opair = to_sibling(z.own.at[1 - core], z.opair, sem.opair)
    opair.start()

    z.mterm[...] = (
        dot_tn(select_cot[:, :RANK], z.half[...]).astype(BF16).reshape(2, CHIPS, 16, C)
    )
    mpair = to_sibling(z.mterm.at[1 - core], z.mpair, sem.mpair)
    mpair.start()
    opair.wait()
    z.ojoin[...] = z.own[core] + z.opair[...]
    sums = Exchange(z.ojoin, z.got_own, sem.own, "chips")
    sums.start()
    z.got_own[chip] = z.ojoin[chip]
    mpair.wait()
    z.msum[...] = (z.mterm[core].astype(F32) + z.mpair[...].astype(F32)).astype(BF16)
    mains = Exchange(z.msum, z.got_m, sem.msum, "chips")
    mains.start()
    z.got_m[chip] = z.msum[chip]

    below.wait()
    z.trail[T:, :] = z.late[...] * (ctx < CTX - 1).astype(F32)
    result = jnp.zeros((T, C), F32)
    for k in range(TAPS):
        result = result + z.taps[k : k + 1, :] * z.trail[pl.ds(TAPS - 1 - k, T), :]
    z.inner_grad[...] = result.astype(BF16)

    sums.wait_recv()
    z.params[core, chip] = jnp.sum(z.got_own[:, 0], axis=0)
    shares = Exchange(z.params.at[core], z.params.at[core], sem.params, "chips", same=True)
    shares.start()
    last = jnp.sum(z.got_own[:, 1], axis=0)
    for k in range(8):
        z.select_grad[16:17, 128 * k : 128 * k + 128] = last[k : k + 1, :]
    for h in range(HALVES):
        deltas[h].wait_recv()
        z.delta_grad[:, h * H : h * H + H] = jnp.sum(z.got_d[h].astype(F32), axis=0)
    for exchange in (ends, home, scatter2, gather2, deltas[0], deltas[1], sums):
        exchange.wait_send()
    shares.wait_recv()
    ppair = to_sibling(z.params.at[core], z.params.at[core], sem.ppair)
    ppair.start()
    mains.wait_recv()
    z.select_grad[0:16, :] = jnp.sum(z.got_m[...].astype(F32), axis=0)
    mains.wait_send()
    shares.wait_send()
    ppair.wait()
    for k in range(8):
        lanes = slice(128 * k, 128 * k + 128)
        z.decay_grad[0:8, lanes] = z.params[0, k]
        z.decay_grad[8:16, lanes] = z.params[0, 8 + k]
        rows = z.params[1, k]
        z.bias_grad[:, lanes] = rows[0:1, :]
        z.skip_grad[:, lanes] = rows[1:2, :]
        z.shift_grad[:, lanes] = rows[2:3, :]
        z.taps_grad[:, lanes] = rows[3:7, :]


def layer(*args):
    return pl.pallas_call(
        layer_kernel,
        out_shape=[jax.ShapeDtypeStruct(shape, kind) for _, shape, kind in OUTPUTS],
        in_specs=[pl.BlockSpec(memory_space=pl.ANY)] * len(INPUTS),
        out_specs=[VMEM] * len(OUTPUTS),
        scratch_shapes=[pltpu.VMEM(shape, kind) for _, shape, kind in INPUTS + SCRATCH]
        + [pltpu.SemaphoreType.DMA(shape) for _, shape in SEMS],
        compiler_params=pltpu.CompilerParams(
            collective_id=0, has_side_effects=True, vmem_limit_bytes=56 << 20
        ),
        name="layer",
    )(*args)


def finish_kernel(*refs):
    count = len(OUTPUTS)
    for given, out in zip(refs[:count], refs[count:]):
        out[...] = given[...]


def finish(*args):
    return pl.pallas_call(
        finish_kernel,
        out_shape=[jax.ShapeDtypeStruct(shape, kind) for _, shape, kind in OUTPUTS],
        in_specs=[VMEM] * len(OUTPUTS),
        out_specs=[VMEM] * len(OUTPUTS),
        name="finish",
    )(*args)


def body(
    inner_in, gate_in, out_grad, kernel, kernel_shift, select_proj, delta_proj, delta_bias,
    decay_log, skip_gain,
):
    parts = layer(
        inner_in, gate_in, out_grad, kernel.T, kernel_shift[None], select_proj, delta_proj,
        delta_bias[None], decay_log.T, skip_gain[None],
    )
    inner_grad, gate_grad, taps, shift, select, delta, bias, decay, skip = finish(*parts)
    return (
        inner_grad, gate_grad, taps.T, shift[0], select, delta.T, bias[0], decay.T, skip[0],
    )


def solution(mesh):
    return jax.shard_map(
        body,
        mesh=mesh,
        in_specs=(
            P("context", "tensor"),
            P("context", "tensor"),
            P("context", "tensor"),
            P("tensor", None),
            P("tensor"),
            P(None, "tensor"),
            P("tensor", None),
            P("tensor"),
            P("tensor", None),
            P("tensor"),
        ),
        out_specs=(
            P("context", "tensor"),
            P("context", "tensor"),
            P("tensor", None),
            P("tensor"),
            P("context", "tensor"),
            P("tensor", "context"),
            P("tensor"),
            P("tensor", None),
            P("tensor"),
        ),
        check_vma=False,
    )
```

```python
import functools

import jax
import jax.numpy as jnp
from jax import lax
from jax.experimental import pallas as pl
from jax.experimental.pallas import tpu as pltpu
from jax.sharding import PartitionSpec as P

CONTEXT, TENSOR, CHIP = "context", "tensor", "chips"
N = 16
RANK = 512
TAPS = 4
PROJ = 544
WIDE = 640
T = 128
C = 1024
H = 512
CTX = 32
TEN = 8
CHIPS = CTX // 2
ROWS = T // TEN
LOG2E = 1.4426950408889634
MESH = pl.DeviceIdType.MESH
F32 = jnp.float32
BF16 = jnp.bfloat16
VMEM = pl.BlockSpec(memory_space=pltpu.VMEM)


def dot_nn(a, b):
    return lax.dot_general(a, b, (((1,), (0,)), ((), ())), preferred_element_type=F32)


def dot_nt(a, b):
    return lax.dot_general(a, b, (((1,), (1,)), ((), ())), preferred_element_type=F32)


def dot_tn(a, b):
    return lax.dot_general(a, b, (((0,), (0,)), ((), ())), preferred_element_type=F32)


def iota(shape, axis):
    return lax.broadcasted_iota(jnp.int32, shape, axis)


def sigmoid(v):
    return jax.nn.sigmoid(v)


def silu_slope(v):
    s = sigmoid(v)
    return s * (1.0 + v * (1.0 - s))


def split_tile(v):
    high = v.astype(BF16).astype(F32)
    return jnp.where(iota(v.shape, 1) < 64, high, v - high).astype(BF16)


def far_first(k, size):
    if isinstance(k, int):
        return size // 2 + (k + 1) // 2 * (1 - 2 * (k % 2))
    return size // 2 + (k + 1) // 2 * (1 - 2 * lax.rem(k, 2))


def peer_of(group, k):
    if group == TENSOR:
        at = lax.axis_index(TENSOR)
        peer = lax.rem(at + far_first(k, TEN), TEN)
        return at, peer, {TENSOR: peer}
    me = lax.axis_index(CONTEXT)
    place, core = (k // 2, 1 - k % 2) if group == CONTEXT else (k, 0)
    x = lax.rem(me // 8 + far_first(place // 4, 4), 4)
    y = lax.rem(me // 2 + far_first(place % 4, 4), 4)
    peer = (x * 4 + y) * 2 + lax.rem(me + core, 2)
    if group == CHIP:
        return me // 2, x * 4 + y, {CONTEXT: peer}
    return me, peer, {CONTEXT: peer}


PEERS = {TENSOR: TEN - 1, CONTEXT: CTX - 1, CHIP: CHIPS - 1}


class Exchange:
    def __init__(self, src, dst, sems, group, same=False):
        self.src, self.dst, self.send, self.recv = src, dst, sems.at[0], sems.at[1]
        self.group, self.same = group, same

    def copy(self, k):
        at, peer, target = peer_of(self.group, k)
        return pltpu.make_async_remote_copy(
            src_ref=self.src.at[at] if self.same else self.src.at[peer],
            dst_ref=self.dst.at[at],
            send_sem=self.send.at[k],
            recv_sem=self.recv.at[k],
            device_id=target,
            device_id_type=MESH,
        )

    def every(self, act):
        lax.fori_loop(0, PEERS[self.group], lambda k, _: (act(self.copy(k)), 0)[1], 0)

    def start(self):
        for k in range(PEERS[self.group]):
            self.copy(k).start()

    def wait_recv(self):
        self.every(lambda copy: copy.wait_recv())

    def wait_send(self):
        self.every(lambda copy: copy.wait_send())

    def to_core(self, core, act):
        other = lax.rem(lax.axis_index(CONTEXT) + core, 2)
        lax.fori_loop(
            0, CHIPS - 1 + other, lambda q, _: (act(self.copy(2 * q + 1 - other)), 0)[1], 0
        )


def greet(group):
    barrier = pltpu.get_barrier_semaphore()

    for k in range(PEERS[group]):
        pl.semaphore_signal(barrier, inc=1, device_id=peer_of(group, k)[2], device_id_type=MESH)


def to_neighbour(src, dst, send, recv, step):
    peer = lax.rem(lax.axis_index(CONTEXT) + step + CTX, CTX)
    return pltpu.make_async_remote_copy(
        src_ref=src, dst_ref=dst, send_sem=send, recv_sem=recv,
        device_id={CONTEXT: peer}, device_id_type=MESH,
    )


def spread(z, tile):
    rows = T * N
    repeat = (iota((rows, T), 0) // N == iota((rows, T), 1)).astype(BF16)
    each = dot_nn(repeat, tile)
    place = iota((rows, 128), 1) % 64 - iota((rows, 128), 0) % N
    unit = jnp.ones((128, 128), BF16)
    z.bspread[...] = dot_nn(jnp.where(place == 0, each, 0.0).astype(BF16), unit).reshape(T, N, 128)
    z.cspread[...] = dot_nn(jnp.where(place == N, each, 0.0).astype(BF16), unit).reshape(T, N, 128)


HALVES = C // H
LT = H // 128

SCRATCH = (
    ("pad", (T + 16, C), F32),
    ("pre", (T, C), F32),
    ("conv", (T, C), F32),
    ("slope", (T, C), F32),
    ("half", (T, C), BF16),
    ("ocot", (T, C), F32),
    ("gslope", (T, C), F32),
    ("sig", (T, C), F32),
    ("deltas", (T, C), F32),
    ("dx", (T, C), F32),
    ("y", (T, C), F32),
    ("along", (T, C), F32),
    ("wsum", (T, C), F32),
    ("direct", (T, C), F32),
    ("halo", (16, C), BF16),
    ("wtail", (128, C), BF16),
    ("part", (TEN, ROWS, WIDE), BF16),
    ("got_part", (TEN, ROWS, WIDE), BF16),
    ("proj", (TEN, ROWS, WIDE), BF16),
    ("bspread", (T, N, 128), F32),
    ("cspread", (T, N, 128), F32),
    ("ends", (CTX, 9, 128), F32),
    ("got_ends", (CTX, 9, 128), F32),
    ("decays", (CTX, 8, 128), F32),
    ("back", (CTX, 8, 128), F32),
    ("borders", (CTX, 8, 128), F32),
    ("before", (T, N, H), F32),
    ("isum", (HALVES, T, N, 128), F32),
    ("osum", (HALVES, T, N, 128), F32),
    ("decay_part", (N, C), F32),
    ("psel", (TEN, ROWS, WIDE), BF16),
    ("got_psel", (TEN, ROWS, WIDE), BF16),
    ("sel", (TEN, ROWS, WIDE), BF16),
    ("order", (WIDE, WIDE), BF16),
    ("fold", (T, T * N), BF16),
    ("dterm", (HALVES, 2, CHIPS, 16, H), BF16),
    ("dpair", (HALVES, CHIPS, 16, H), BF16),
    ("dsum", (HALVES, CHIPS, 16, H), BF16),
    ("got_d", (HALVES, CHIPS, 16, H), BF16),
    ("mterm", (HALVES, 2, CHIPS, 16, H), BF16),
    ("mpair", (HALVES, CHIPS, 16, H), BF16),
    ("msum", (HALVES, CHIPS, 16, H), BF16),
    ("got_m", (HALVES, CHIPS, 16, H), BF16),
    ("early", (2, CHIPS, 8, 128), F32),
    ("epair", (CHIPS, 8, 128), F32),
    ("ejoin", (CHIPS, 8, 128), F32),
    ("got_early", (CHIPS, 8, 128), F32),
    ("params", (2, CHIPS, 8, 128), F32),
    ("own", (2, CHIPS, 16, 384), BF16),
    ("opair", (CHIPS, 16, 384), BF16),
    ("ojoin", (CHIPS, 16, 384), BF16),
    ("got_own", (CHIPS, 16, 384), BF16),
    ("late_sums", (2, 8, H), F32),
    ("wdperm", (C, WIDE), BF16),
    ("wsperm", (WIDE, C), BF16),
    ("trail", (T + 8, C), F32),
    ("edge", (8, C), F32),
    ("late", (8, C), F32),
)
INPUTS = (
    ("inner", (T, C), BF16),
    ("gate", (T, C), BF16),
    ("grad", (T, C), BF16),
    ("taps", (TAPS, C), F32),
    ("shift", (1, C), F32),
    ("wsel", (PROJ, C), BF16),
    ("wdelta", (C, RANK), BF16),
    ("bias", (1, C), F32),
    ("dlog", (N, C), F32),
    ("skip", (1, C), F32),
)
OUTPUTS = (
    ("inner_grad", (T, C), BF16),
    ("gate_grad", (T, C), BF16),
    ("taps_grad", (TAPS, C), F32),
    ("shift_grad", (1, C), F32),
    ("select_grad", (17, C), F32),
    ("delta_grad", (16, C), F32),
    ("bias_grad", (1, C), F32),
    ("decay_grad", (N, C), F32),
    ("skip_grad", (1, C), F32),
)
SEMS = (
    ("in", (len(INPUTS),)),
    ("halo", (2,)),
    ("part", (2, TEN)),
    ("proj", (2, TEN)),
    ("ends", (2, CTX)),
    ("back", (2, CTX)),
    ("psel", (2, TEN)),
    ("sel", (2, TEN)),
    ("dpair", (HALVES, 2)),
    ("dsum", (HALVES, 2, CHIPS)),
    ("mpair", (HALVES, 2)),
    ("msum", (HALVES, 2, CHIPS)),
    ("epair", (2,)),
    ("early", (2, CHIPS)),
    ("params", (2, CHIPS)),
    ("ppair", (2,)),
    ("opair", (2,)),
    ("own", (2, CHIPS)),
    ("lpair", (2,)),
    ("edge", (2,)),
)


class Refs:
    pass


def tile_of(v, r, k):
    return v[8 * r : 8 * r + 8, 128 * k : 128 * k + 128]


def wide_of(v):
    return jnp.concatenate([v] * LT, 1)


def lane_sum(v):
    return functools.reduce(jnp.add, [v[:, 128 * k : 128 * k + 128] for k in range(LT)])


def half_lanes(h):
    return pl.ds(pl.multiple_of(h * H, H), H)


def convolve(z, first, rows):
    value = jnp.zeros((rows, C), F32) + z.shift[...]
    for k in range(TAPS):
        value = value + z.taps[k : k + 1, :] * z.pad[pl.ds(first + 16 - TAPS + 1 + k, rows), :]
    z.pre[pl.ds(first, rows), :] = value
    s = sigmoid(value)
    conv = value * s
    z.conv[pl.ds(first, rows), :] = conv
    z.half[pl.ds(first, rows), :] = conv.astype(BF16)
    z.slope[pl.ds(first, rows), :] = s * (1.0 + value * (1.0 - s))


def project(z, first, rows):
    half = z.half[pl.ds(first, rows), :]
    blocks = pl.ds(first // ROWS, rows // ROWS)
    shape = (rows // ROWS, ROWS)
    z.part[blocks, :, :RANK] = dot_nt(half, z.wsel[:RANK, :]).astype(BF16).reshape(*shape, RANK)
    z.part[blocks, :, RANK:] = split_tile(dot_nt(half, z.wtail[...])).reshape(*shape, 128)


def border_at(direction, r, k, h):
    return (direction * 8 + r * LT + k) * 2 + h


def summarize(z, h, lengths):
    lanes = slice(h * H, h * H + H)
    rate = jnp.exp(z.dlog[:, lanes]) * (-LOG2E)

    def steps(block, carried):
        state, decay, flow = carried
        for i in range(8):
            t = block * 8 + i
            row = pl.ds(t, 1)
            d = jnp.exp2(z.deltas[row, lanes] * rate)
            state = d * state + z.dx[row, lanes] * wide_of(z.bspread[t])
            decay = decay * d
            flow = flow + decay * (z.ocot[row, lanes] * wide_of(z.cspread[t]))
        return state, decay, flow

    zero = jnp.zeros((N, H), F32)
    state, _, flow = lax.fori_loop(0, T // 8, steps, (zero, zero + 1.0, zero))
    for r in range(N // 8):
        for k in range(LT):
            for direction, value in enumerate((state, flow)):
                at = border_at(direction, r, k, h)
                z.ends[at, 0:8, :] = tile_of(value, r, k)
                z.ends[at, 8:9, :] = lengths[:, h * H + 128 * k : h * H + 128 * k + 128]


def edges(z, direction, h):
    return jnp.concatenate(
        [
            jnp.concatenate([z.borders[border_at(direction, r, k, h)] for k in range(LT)], 1)
            for r in range(N // 8)
        ],
        0,
    )


class Fold:
    def __init__(self, rising):
        self.rising, self.waiting = rising, {}

    def push(self, value):
        value, step = value[0:8, :] + value[8:16, :], 1
        sub = iota(value.shape, 0)
        while step in self.waiting:
            other = self.waiting.pop(step)
            a, b = (other, value) if self.rising else (value, other)
            low = sub // step % 2 == 0
            value = jnp.where(low, a, b) + pltpu.roll(jnp.where(low, b, a), step, 0)
            step *= 2
        self.waiting[step] = value

    def result(self):
        return self.waiting[8]


def rows_of8(block):
    return pl.ds(pl.multiple_of(block * 8, 8), 8)


def go_forward(z, h):
    lanes = slice(h * H, h * H + H)
    rate2 = jnp.exp(z.dlog[:, lanes]) * (-LOG2E)

    def forward(block, state):
        y = Fold(True)
        for i in range(8):
            t = block * 8 + i
            row = pl.ds(t, 1)
            z.before[t] = state
            d = jnp.exp2(z.deltas[row, lanes] * rate2)
            state = d * state + z.dx[row, lanes] * wide_of(z.bspread[t])
            y.push(state * wide_of(z.cspread[t]))
            z.osum[h, t] = lane_sum(state * z.ocot[row, lanes])
        z.y[rows_of8(block), lanes] = y.result()
        return state

    lax.fori_loop(0, T // 8, forward, edges(z, 0, h))


def go_backward(z, h):
    lanes = slice(h * H, h * H + H)
    rate2 = jnp.exp(z.dlog[:, lanes]) * (-LOG2E)

    def backward(index, carried):
        flow, total = carried
        block = T // 8 - 1 - index
        along, wsum = Fold(False), Fold(False)
        for i in reversed(range(8)):
            t = block * 8 + i
            row = pl.ds(t, 1)
            delta = z.deltas[row, lanes]
            adjoint = z.ocot[row, lanes] * wide_of(z.cspread[t]) + flow
            z.isum[h, t] = lane_sum(adjoint * z.dx[row, lanes])
            along.push(adjoint * wide_of(z.bspread[t]))
            flow = jnp.exp2(delta * rate2) * adjoint
            weighted = flow * z.before[t]
            total = total + weighted * delta
            wsum.push(weighted * rate2)
        z.along[rows_of8(block), lanes] = along.result()
        z.wsum[rows_of8(block), lanes] = wsum.result() * (1.0 / LOG2E)
        return flow, total

    _, total = lax.fori_loop(0, T // 8, backward, (edges(z, 1, h), jnp.zeros((N, H), F32)))
    z.decay_part[:, lanes] = total * (rate2 * (1.0 / LOG2E))


def gather_sums(z):
    unit = jnp.ones((128, 128), BF16)
    place = iota((T * N, 128), 1) - iota((T * N, 128), 0) % N

    def summed(parts):
        return dot_nn((parts[0] + parts[1]).reshape(T * N, 128).astype(BF16), unit)

    both = jnp.where(
        place == 0, summed(z.isum), jnp.where(place == N, summed(z.osum), 0.0)
    ).astype(BF16)
    return dot_nn(z.fold[...], both)


def to_sibling(src, dst, sems):
    me = lax.axis_index(CONTEXT)
    return pltpu.make_async_remote_copy(
        src_ref=src, dst_ref=dst, send_sem=sems.at[0], recv_sem=sems.at[1],
        device_id={CONTEXT: me + 1 - 2 * lax.rem(me, 2)}, device_id_type=MESH,
    )


def send_halves(z, sems, joined, own, other, got, h, pair):
    chip, core = lax.axis_index(CONTEXT) // 2, lax.rem(lax.axis_index(CONTEXT), 2)
    joined, own, other, got = (getattr(z, name) for name in (joined, own, other, got))
    pair.wait()
    joined[h] = (own[h, core].astype(F32) + other[h].astype(F32)).astype(BF16)
    sent = Exchange(joined.at[h], got.at[h], sems.at[h], CHIP)
    sent.start()
    got[h, chip] = joined[h, chip]
    return sent


def layer_kernel(*refs):
    z, given, sem = Refs(), Refs(), Refs()
    refs = list(refs)
    for name, _, _ in INPUTS:
        setattr(given, name, refs.pop(0))
    for name, _, _ in OUTPUTS + INPUTS + SCRATCH:
        setattr(z, name, refs.pop(0))
    for name, _ in SEMS:
        setattr(sem, name, refs.pop(0))
    ctx, ten = lax.axis_index(CONTEXT), lax.axis_index(TENSOR)
    chip, core = ctx // 2, lax.rem(ctx, 2)

    greet(CONTEXT)
    greet(TENSOR)
    loads = {}
    for i, (name, _, _) in enumerate(INPUTS):
        loads[name] = pltpu.make_async_copy(
            getattr(given, name), getattr(z, name), getattr(sem, "in").at[i]
        )

    for name in ("inner", "taps", "shift", "wsel", "gate", "grad", "dlog", "wdelta", "bias", "skip"):
        loads[name].start()

    for name in ("inner", "taps", "shift"):
        loads[name].wait()
    z.pad[16:, :] = z.inner[...].astype(F32)
    convolve(z, 16, T - 16)
    pl.semaphore_wait(pltpu.get_barrier_semaphore(), TEN - 1 + CTX - 1)
    halo = to_neighbour(z.inner.at[pl.ds(T - 16, 16)], z.halo, sem.halo.at[0], sem.halo.at[1], 1)
    halo.start()
    loads["wsel"].wait()
    tail = z.wsel[RANK:PROJ, :]
    z.wtail[0:32, :] = tail
    z.wtail[32:64, :] = jnp.zeros((32, C), BF16)
    z.wtail[64:96, :] = tail
    z.wtail[96:128, :] = jnp.zeros((32, C), BF16)
    project(z, 16, T - 16)
    halo.wait()
    z.pad[0:16, :] = z.halo[...].astype(F32) * (ctx > 0).astype(F32)
    convolve(z, 0, 16)
    project(z, 0, 16)
    scatter = Exchange(z.part, z.got_part, sem.part, TENSOR)
    scatter.start()
    z.got_part[ten] = z.part[ten]

    loads["gate"].wait()
    loads["grad"].wait()
    g = z.gate[...].astype(F32)
    s = sigmoid(g)
    grad = z.grad[...].astype(F32)
    z.ocot[...] = grad * (g * s)
    z.gslope[...] = grad * (s * (1.0 + g * (1.0 - s)))

    scatter.wait_recv()
    total = jnp.sum(z.got_part[...].astype(F32), axis=0)
    bc = total[:, RANK:]
    bc = bc + pltpu.roll(bc, 64, 1)
    z.proj[ten, :, :RANK] = total[:, :RANK].astype(BF16)
    z.proj[ten, :, RANK:] = split_tile(bc)
    gather = Exchange(
        z.proj, z.proj, sem.proj, TENSOR, same=True
    )
    gather.start()
    target = iota((WIDE, WIDE), 0)
    source = iota((WIDE, WIDE), 1)
    place = target % 256
    rest = target - RANK
    order = jnp.where(
        target < RANK,
        (place // 16 * 2 + target // 256) * 17 + place % 16,
        (rest % 16 * 2 + rest // 16) * 17 + 16,
    )
    order = ((order == source) & (target < PROJ)).astype(BF16)
    z.order[...] = order
    loads["wdelta"].wait()
    z.wdperm[...] = dot_nt(z.wdelta[...], order[:, :RANK]).astype(BF16)
    z.wsperm[...] = dot_nn(order[:, :PROJ], z.wsel[...]).astype(BF16)
    z.fold[...] = (iota((T, T * N), 0) == iota((T, T * N), 1) // N).astype(BF16)
    for name in ("dlog", "bias", "skip"):
        loads[name].wait()
    gather.wait_recv()

    flat = z.proj[...].reshape(T, WIDE)
    raw = dot_nt(flat[:, :RANK], z.wdelta[...]) + z.bias[...]
    step = jnp.maximum(raw, 0.0) + jnp.log1p(jnp.exp(-jnp.abs(raw)))
    z.deltas[...] = step
    lengths = jnp.sum(step, axis=0, keepdims=True)
    z.sig[...] = sigmoid(raw)
    z.dx[...] = step * z.conv[...]
    spread(z, flat[:, RANK:])
    ends = Exchange(z.ends, z.got_ends, sem.ends, CONTEXT)
    for h in range(HALVES):
        summarize(z, h, lengths)
        ends.to_core(h, lambda copy: copy.start())

    z.got_ends[ctx] = z.ends[ctx]
    backward = chip // 8
    at_row = pl.ds(pl.multiple_of(lax.rem(chip, 8) // LT * 8, 8), 8)
    at_lane = core * LT + lax.rem(chip, LT)
    rate = jnp.exp(z.dlog[at_row, pl.ds(pl.multiple_of(at_lane * 128, 128), 128)]) * (-LOG2E)
    ends.wait_recv()
    z.decays[...] = jnp.exp2(rate[None] * z.got_ends[:, 8:9, :])
    carried = jnp.zeros((8, 128), F32)
    for i in range(CTX):
        at = i + backward * (CTX - 1 - 2 * i)
        z.back[at] = carried
        carried = z.decays[at] * carried + z.got_ends[at, 0:8, :]
    home = Exchange(z.back, z.borders, sem.back, CONTEXT)
    home.start()
    z.borders[ctx] = z.back[ctx]
    scatter.wait_send()
    gather.wait_send()

    select_part = jnp.zeros((T, WIDE), F32)
    dpairs, deltas, sides = [], [], []
    for h in range(HALVES):
        lanes = slice(h * H, h * H + H)
        home.to_core(h, lambda copy: copy.wait_recv())
        go_forward(z, h)
        if h > 0:
            deltas.append(
                send_halves(z, sem.dsum, "dsum", "dterm", "dpair", "got_d", h - 1, dpairs[h - 1])
            )
        go_backward(z, h)
        near = z.along[:, lanes]
        raw_cot = (z.wsum[:, lanes] + z.conv[:, lanes] * near) * z.sig[:, lanes]
        raw_half = raw_cot.astype(BF16)
        select_part = select_part + dot_nn(raw_half, z.wdperm[lanes, :])
        if h == HALVES - 1:
            select_part = select_part + dot_nt(gather_sums(z).astype(BF16), z.order[:, RANK:])
            z.psel[...] = select_part.astype(BF16).reshape(TEN, ROWS, WIDE)
            scatter2 = Exchange(z.psel, z.got_psel, sem.psel, TENSOR)
            scatter2.start()
            z.got_psel[ten] = z.psel[ten]
        term = dot_tn(flat[:, :RANK], raw_half).astype(BF16).reshape(CHIPS, 2, 16, H)
        z.dterm[h, 0] = term[:, 0]
        z.dterm[h, 1] = term[:, 1]
        dpairs.append(to_sibling(z.dterm.at[h, 1 - core], z.dpair.at[h], sem.dpair.at[h]))
        dpairs[h].start()
        cot, gain, conv = z.ocot[:, lanes], z.skip[:, lanes], z.conv[:, lanes]
        z.gate_grad[:, lanes] = (
            z.gslope[:, lanes] * (z.y[:, lanes] + gain * conv)
        ).astype(BF16)
        z.direct[:, lanes] = gain * cot + z.deltas[:, lanes] * near
        sides.append(
            jnp.concatenate(
                [
                    jnp.sum(raw_cot, axis=0, keepdims=True),
                    jnp.sum(cot * conv, axis=0, keepdims=True),
                ],
                0,
            )
        )

    for k in range(8):
        lanes = slice(128 * k, 128 * k + 128)
        z.early[0, k] = z.decay_part[0:8, lanes]
        z.early[1, k] = z.decay_part[8:16, lanes]
        z.early[:, 8 + k] = jnp.zeros((2, 8, 128), F32)
    epair = to_sibling(z.early.at[1 - core], z.epair, sem.epair)
    epair.start()
    epair.wait()
    z.ejoin[...] = z.early[core] + z.epair[...]
    earlies = Exchange(z.ejoin, z.got_early, sem.early, CHIP)
    earlies.start()
    z.got_early[chip] = z.ejoin[chip]
    scatter2.wait_recv()
    z.sel[ten] = jnp.sum(z.got_psel[...].astype(F32), axis=0).astype(BF16)
    gather2 = Exchange(z.sel, z.sel, sem.sel, TENSOR, same=True)
    gather2.start()
    deltas.append(send_halves(z, sem.dsum, "dsum", "dterm", "dpair", "got_d", 1, dpairs[1]))
    early = jnp.concatenate(sides, 1)
    earlies.wait_recv()
    z.params[core, chip] = jnp.sum(z.got_early[...], axis=0)
    shares = Exchange(z.params.at[core], z.params.at[core], sem.params, CHIP, same=True)
    shares.start()
    gather2.wait_recv()
    select_cot = z.sel[...].reshape(T, WIDE)

    mpairs, mains = [], []
    for h in range(HALVES):
        term = dot_tn(select_cot[:, :RANK], z.half[:, h * H : h * H + H]).astype(BF16)
        z.mterm[h] = term.reshape(2, CHIPS, 16, H)
        mpairs.append(to_sibling(z.mterm.at[h, 1 - core], z.mpair.at[h], sem.mpair.at[h]))
        mpairs[h].start()

    pre_cot = (z.direct[...] + dot_nn(select_cot, z.wsperm[...])) * z.slope[...]
    z.trail[0:T, :] = pre_cot
    z.edge[...] = pre_cot[0:8, :]
    below = to_neighbour(z.edge, z.late, sem.edge.at[0], sem.edge.at[1], -1)
    below.start()
    rows = [early, jnp.sum(pre_cot, axis=0, keepdims=True)]
    for k in range(TAPS):
        rows.append(
            jnp.sum(pre_cot * z.pad[pl.ds(16 - TAPS + 1 + k, T), :], axis=0, keepdims=True)
        )
    rows = jnp.concatenate(rows + [jnp.zeros((1, C), F32)], 0)
    extra = dot_tn(select_cot[:, RANK:], z.half[...])
    for d in range(2):
        mine = jnp.concatenate(
            [rows[:, d * H : d * H + 256], rows[:, d * H + 256 : d * H + 512]], 0
        ).astype(BF16)
        for c in range(CHIPS):
            row = extra[d * CHIPS + c : d * CHIPS + c + 1, :]
            tile = jnp.concatenate(
                [row[:, 128 * k : 128 * k + 128] for k in range(8)] + [jnp.zeros((8, 128), F32)], 0
            )
            z.own[d, c, :, 0:256] = mine
            z.own[d, c, :, 256:384] = tile.astype(BF16)
    opair = to_sibling(z.own.at[1 - core], z.opair, sem.opair)
    opair.start()
    mains.append(send_halves(z, sem.msum, "msum", "mterm", "mpair", "got_m", 0, mpairs[0]))
    opair.wait()
    z.ojoin[...] = (z.own[core].astype(F32) + z.opair[...].astype(F32)).astype(BF16)
    sums = Exchange(z.ojoin, z.got_own, sem.own, CHIP)
    sums.start()
    z.got_own[chip] = z.ojoin[chip]
    mains.append(send_halves(z, sem.msum, "msum", "mterm", "mpair", "got_m", 1, mpairs[1]))

    shares.wait_recv()
    ppair = to_sibling(z.params.at[core], z.params.at[core], sem.ppair)
    ppair.start()
    below.wait()
    z.trail[T:, :] = z.late[...] * (ctx < CTX - 1).astype(F32)
    result = jnp.zeros((T, C), F32)
    for k in range(TAPS):
        result = result + z.taps[k : k + 1, :] * z.trail[pl.ds(TAPS - 1 - k, T), :]
    z.inner_grad[...] = result.astype(BF16)
    for h in range(HALVES):
        deltas[h].wait_recv()
        z.delta_grad[:, h * H : h * H + H] = jnp.sum(z.got_d[h].astype(F32), axis=0)
    ppair.wait()
    for k in range(8):
        lanes = slice(128 * k, 128 * k + 128)
        z.decay_grad[0:8, lanes] = z.params[0, k]
        z.decay_grad[8:16, lanes] = z.params[1, k]
    for exchange in (ends, home, scatter2, gather2, deltas[0], deltas[1], earlies, shares):
        exchange.wait_send()

    sums.wait_recv()
    both = jnp.sum(z.got_own[...].astype(F32), axis=0)
    z.late_sums[core] = jnp.concatenate([both[0:8, 0:256], both[8:16, 0:256]], 1)
    lpair = to_sibling(z.late_sums.at[core], z.late_sums.at[core], sem.lpair)
    lpair.start()
    for k in range(8):
        z.select_grad[16:17, 128 * k : 128 * k + 128] = both[k : k + 1, 256:384]
    for exchange in (sums, mains[0], mains[1]):
        exchange.wait_send()
    for h in range(HALVES):
        mains[h].wait_recv()
        z.select_grad[0:16, h * H : h * H + H] = jnp.sum(z.got_m[h].astype(F32), axis=0)
    lpair.wait()
    for d in range(2):
        lanes = slice(d * H, d * H + H)
        rows = z.late_sums[d]
        z.bias_grad[:, lanes] = rows[0:1, :]
        z.skip_grad[:, lanes] = rows[1:2, :]
        z.shift_grad[:, lanes] = rows[2:3, :]
        z.taps_grad[:, lanes] = rows[3:7, :]


def layer(*args):
    return pl.pallas_call(
        layer_kernel,
        out_shape=[jax.ShapeDtypeStruct(shape, kind) for _, shape, kind in OUTPUTS],
        in_specs=[pl.BlockSpec(memory_space=pl.ANY)] * len(INPUTS),
        out_specs=[VMEM] * len(OUTPUTS),
        scratch_shapes=[pltpu.VMEM(shape, kind) for _, shape, kind in INPUTS + SCRATCH]
        + [pltpu.SemaphoreType.DMA(shape) for _, shape in SEMS],
        compiler_params=pltpu.CompilerParams(
            collective_id=0, has_side_effects=True, vmem_limit_bytes=56 << 20
        ),
        name="layer",
    )(*args)


def finish_kernel(*refs):
    count = len(OUTPUTS)
    for given, out in zip(refs[:count], refs[count:]):
        out[...] = given[...]


def finish(*args):
    return pl.pallas_call(
        finish_kernel,
        out_shape=[jax.ShapeDtypeStruct(shape, kind) for _, shape, kind in OUTPUTS],
        in_specs=[VMEM] * len(OUTPUTS),
        out_specs=[VMEM] * len(OUTPUTS),
        name="finish",
    )(*args)


def body(
    inner_in, gate_in, out_grad, kernel, kernel_shift, select_proj, delta_proj, delta_bias,
    decay_log, skip_gain,
):
    parts = layer(
        inner_in, gate_in, out_grad, kernel.T, kernel_shift[None], select_proj, delta_proj,
        delta_bias[None], decay_log.T, skip_gain[None],
    )
    inner_grad, gate_grad, taps, shift, select, delta, bias, decay, skip = finish(*parts)
    return (
        inner_grad, gate_grad, taps.T, shift[0], select, delta.T, bias[0], decay.T, skip[0],
    )


def solution(mesh):
    return jax.shard_map(
        body,
        mesh=mesh,
        in_specs=(
            P(CONTEXT, TENSOR),
            P(CONTEXT, TENSOR),
            P(CONTEXT, TENSOR),
            P(TENSOR, None),
            P(TENSOR),
            P(None, TENSOR),
            P(TENSOR, None),
            P(TENSOR),
            P(TENSOR, None),
            P(TENSOR),
        ),
        out_specs=(
            P(CONTEXT, TENSOR),
            P(CONTEXT, TENSOR),
            P(TENSOR, None),
            P(TENSOR),
            P(CONTEXT, TENSOR),
            P(TENSOR, CONTEXT),
            P(TENSOR),
            P(TENSOR, None),
            P(TENSOR),
        ),
        check_vma=False,
    )
```

```python
import functools

import jax
import jax.numpy as jnp
from jax import lax
from jax.experimental import pallas as pl
from jax.experimental.pallas import tpu as pltpu
from jax.sharding import PartitionSpec as P

CONTEXT, TENSOR, CHIP = "context", "tensor", "chips"
N = 16
RANK = 512
TAPS = 4
PROJ = 544
WIDE = 640
T = 128
C = 1024
H = 512
CTX = 32
TEN = 8
CHIPS = CTX // 2
ROWS = T // TEN
LOG2E = 1.4426950408889634
MESH = pl.DeviceIdType.MESH
F32 = jnp.float32
BF16 = jnp.bfloat16
VMEM = pl.BlockSpec(memory_space=pltpu.VMEM)


def dot_nn(a, b):
    return lax.dot_general(a, b, (((1,), (0,)), ((), ())), preferred_element_type=F32)


def dot_nt(a, b):
    return lax.dot_general(a, b, (((1,), (1,)), ((), ())), preferred_element_type=F32)


def dot_tn(a, b):
    return lax.dot_general(a, b, (((0,), (0,)), ((), ())), preferred_element_type=F32)


def iota(shape, axis):
    return lax.broadcasted_iota(jnp.int32, shape, axis)


def sigmoid(v):
    return jax.nn.sigmoid(v)


def silu_slope(v):
    s = sigmoid(v)
    return s * (1.0 + v * (1.0 - s))


def split_tile(v):
    high = v.astype(BF16).astype(F32)
    return jnp.where(iota(v.shape, 1) < 64, high, v - high).astype(BF16)


def far_first(k, size):
    if isinstance(k, int):
        return size // 2 + (k + 1) // 2 * (1 - 2 * (k % 2))
    return size // 2 + (k + 1) // 2 * (1 - 2 * lax.rem(k, 2))


def peer_of(group, k):
    if group == TENSOR:
        at = lax.axis_index(TENSOR)
        peer = lax.rem(at + far_first(k, TEN), TEN)
        return at, peer, {TENSOR: peer}
    me = lax.axis_index(CONTEXT)
    place, core = (k // 2, 1 - k % 2) if group == CONTEXT else (k, 0)
    x = lax.rem(me // 8 + far_first(place // 4, 4), 4)
    y = lax.rem(me // 2 + far_first(place % 4, 4), 4)
    peer = (x * 4 + y) * 2 + lax.rem(me + core, 2)
    if group == CHIP:
        return me // 2, x * 4 + y, {CONTEXT: peer}
    return me, peer, {CONTEXT: peer}


PEERS = {TENSOR: TEN - 1, CONTEXT: CTX - 1, CHIP: CHIPS - 1}


class Exchange:
    def __init__(self, src, dst, sems, group, same=False):
        self.src, self.dst, self.send, self.recv = src, dst, sems.at[0], sems.at[1]
        self.group, self.same = group, same

    def copy(self, k):
        at, peer, target = peer_of(self.group, k)
        return pltpu.make_async_remote_copy(
            src_ref=self.src.at[at] if self.same else self.src.at[peer],
            dst_ref=self.dst.at[at],
            send_sem=self.send.at[k],
            recv_sem=self.recv.at[k],
            device_id=target,
            device_id_type=MESH,
        )

    def every(self, act):
        lax.fori_loop(0, PEERS[self.group], lambda k, _: (act(self.copy(k)), 0)[1], 0)

    def start(self):
        for k in range(PEERS[self.group]):
            self.copy(k).start()

    def wait_recv(self):
        self.every(lambda copy: copy.wait_recv())

    def wait_send(self):
        self.every(lambda copy: copy.wait_send())

    def to_core(self, core, act):
        other = lax.rem(lax.axis_index(CONTEXT) + core, 2)
        lax.fori_loop(
            0, CHIPS - 1 + other, lambda q, _: (act(self.copy(2 * q + 1 - other)), 0)[1], 0
        )


def greet(group):
    barrier = pltpu.get_barrier_semaphore()

    for k in range(PEERS[group]):
        pl.semaphore_signal(barrier, inc=1, device_id=peer_of(group, k)[2], device_id_type=MESH)


def to_neighbour(src, dst, send, recv, step):
    peer = lax.rem(lax.axis_index(CONTEXT) + step + CTX, CTX)
    return pltpu.make_async_remote_copy(
        src_ref=src, dst_ref=dst, send_sem=send, recv_sem=recv,
        device_id={CONTEXT: peer}, device_id_type=MESH,
    )


def spread(z, tile):
    rows = T * N
    repeat = (iota((rows, T), 0) // N == iota((rows, T), 1)).astype(BF16)
    each = dot_nn(repeat, tile)
    place = iota((rows, 128), 1) % 64 - iota((rows, 128), 0) % N
    unit = jnp.ones((128, 128), BF16)
    z.bspread[...] = dot_nn(jnp.where(place == 0, each, 0.0).astype(BF16), unit).reshape(T, N, 128)
    z.cspread[...] = dot_nn(jnp.where(place == N, each, 0.0).astype(BF16), unit).reshape(T, N, 128)


HALVES = C // H
LT = H // 128

SCRATCH = (
    ("pad", (T + 16, C), F32),
    ("pre", (T, C), F32),
    ("conv", (T, C), F32),
    ("slope", (T, C), F32),
    ("half", (T, C), BF16),
    ("ocot", (T, C), F32),
    ("gslope", (T, C), F32),
    ("sig", (T, C), F32),
    ("deltas", (T, C), F32),
    ("dx", (T, C), F32),
    ("y", (T, C), F32),
    ("along", (T, C), F32),
    ("wsum", (T, C), F32),
    ("direct", (T, C), F32),
    ("halo", (16, C), BF16),
    ("wtail", (128, C), BF16),
    ("part", (TEN, ROWS, WIDE), BF16),
    ("got_part", (TEN, ROWS, WIDE), BF16),
    ("proj", (TEN, ROWS, WIDE), BF16),
    ("bspread", (T, N, 128), F32),
    ("cspread", (T, N, 128), F32),
    ("ends", (CTX, 9, 128), F32),
    ("got_ends", (CTX, 9, 128), F32),
    ("decays", (CTX, 8, 128), F32),
    ("back", (CTX, 8, 128), F32),
    ("borders", (CTX, 8, 128), F32),
    ("before", (T, N, H), F32),
    ("isum", (HALVES, T, N, 128), F32),
    ("osum", (HALVES, T, N, 128), F32),
    ("decay_part", (N, C), F32),
    ("psel", (TEN, ROWS, WIDE), BF16),
    ("got_psel", (TEN, ROWS, WIDE), BF16),
    ("sel", (TEN, ROWS, WIDE), BF16),
    ("order", (WIDE, WIDE), BF16),
    ("fold", (T, T * N), BF16),
    ("dterm", (HALVES, 2, CHIPS, 16, H), BF16),
    ("dpair", (HALVES, CHIPS, 16, H), BF16),
    ("dsum", (HALVES, CHIPS, 16, H), BF16),
    ("got_d", (HALVES, CHIPS, 16, H), BF16),
    ("mterm", (HALVES, 2, CHIPS, 16, H), BF16),
    ("mpair", (HALVES, CHIPS, 16, H), BF16),
    ("msum", (HALVES, CHIPS, 16, H), BF16),
    ("got_m", (HALVES, CHIPS, 16, H), BF16),
    ("early", (2, CHIPS, 8, 128), F32),
    ("epair", (CHIPS, 8, 128), F32),
    ("ejoin", (CHIPS, 8, 128), F32),
    ("got_early", (CHIPS, 8, 128), F32),
    ("params", (2, CHIPS, 8, 128), F32),
    ("own", (2, CHIPS, 16, 384), BF16),
    ("opair", (CHIPS, 16, 384), BF16),
    ("ojoin", (CHIPS, 16, 384), BF16),
    ("got_own", (CHIPS, 16, 384), BF16),
    ("late_sums", (2, 8, H), F32),
    ("wdperm", (C, WIDE), BF16),
    ("wsperm", (WIDE, C), BF16),
    ("trail", (T + 8, C), F32),
    ("edge", (8, C), F32),
    ("late", (8, C), F32),
)
INPUTS = (
    ("inner", (T, C), BF16),
    ("gate", (T, C), BF16),
    ("grad", (T, C), BF16),
    ("taps", (TAPS, C), F32),
    ("shift", (1, C), F32),
    ("wsel", (PROJ, C), BF16),
    ("wdelta", (C, RANK), BF16),
    ("bias", (1, C), F32),
    ("dlog", (N, C), F32),
    ("skip", (1, C), F32),
)
OUTPUTS = (
    ("inner_grad", (T, C), BF16),
    ("gate_grad", (T, C), BF16),
    ("taps_grad", (TAPS, C), F32),
    ("shift_grad", (1, C), F32),
    ("select_grad", (17, C), F32),
    ("delta_grad", (16, C), F32),
    ("bias_grad", (1, C), F32),
    ("decay_grad", (N, C), F32),
    ("skip_grad", (1, C), F32),
)
SEMS = (
    ("in", (len(INPUTS),)),
    ("halo", (2,)),
    ("part", (2, TEN)),
    ("proj", (2, TEN)),
    ("ends", (2, CTX)),
    ("back", (2, CTX)),
    ("psel", (2, TEN)),
    ("sel", (2, TEN)),
    ("dpair", (HALVES, 2)),
    ("dsum", (HALVES, 2, CHIPS)),
    ("mpair", (HALVES, 2)),
    ("msum", (HALVES, 2, CHIPS)),
    ("epair", (2,)),
    ("early", (2, CHIPS)),
    ("params", (2, CHIPS)),
    ("ppair", (2,)),
    ("opair", (2,)),
    ("own", (2, CHIPS)),
    ("lpair", (2,)),
    ("edge", (2,)),
)


class Refs:
    pass


def tile_of(v, r, k):
    return v[8 * r : 8 * r + 8, 128 * k : 128 * k + 128]


def wide_of(v):
    return jnp.concatenate([v] * LT, 1)


def lane_sum(v):
    return functools.reduce(jnp.add, [v[:, 128 * k : 128 * k + 128] for k in range(LT)])


def half_lanes(h):
    return pl.ds(pl.multiple_of(h * H, H), H)


def convolve(z, first, rows):
    value = jnp.zeros((rows, C), F32) + z.shift[...]
    for k in range(TAPS):
        value = value + z.taps[k : k + 1, :] * z.pad[pl.ds(first + 16 - TAPS + 1 + k, rows), :]
    z.pre[pl.ds(first, rows), :] = value
    s = sigmoid(value)
    conv = value * s
    z.conv[pl.ds(first, rows), :] = conv
    z.half[pl.ds(first, rows), :] = conv.astype(BF16)
    z.slope[pl.ds(first, rows), :] = s * (1.0 + value * (1.0 - s))


def project(z, first, rows):
    half = z.half[pl.ds(first, rows), :]
    blocks = pl.ds(first // ROWS, rows // ROWS)
    shape = (rows // ROWS, ROWS)
    z.part[blocks, :, :RANK] = dot_nt(half, z.wsel[:RANK, :]).astype(BF16).reshape(*shape, RANK)
    z.part[blocks, :, RANK:] = split_tile(dot_nt(half, z.wtail[...])).reshape(*shape, 128)


def border_at(direction, r, k, h):
    return (direction * 8 + r * LT + k) * 2 + h


def summarize(z, h, lengths):
    lanes = slice(h * H, h * H + H)
    rate = jnp.exp(z.dlog[:, lanes]) * (-LOG2E)

    def steps(block, carried):
        state, decay, flow = carried
        for i in range(8):
            t = block * 8 + i
            row = pl.ds(t, 1)
            d = jnp.exp2(z.deltas[row, lanes] * rate)
            state = d * state + z.dx[row, lanes] * wide_of(z.bspread[t])
            decay = decay * d
            flow = flow + decay * (z.ocot[row, lanes] * wide_of(z.cspread[t]))
        return state, decay, flow

    zero = jnp.zeros((N, H), F32)
    state, _, flow = lax.fori_loop(0, T // 8, steps, (zero, zero + 1.0, zero))
    for r in range(N // 8):
        for k in range(LT):
            for direction, value in enumerate((state, flow)):
                at = border_at(direction, r, k, h)
                z.ends[at, 0:8, :] = tile_of(value, r, k)
                z.ends[at, 8:9, :] = lengths[:, h * H + 128 * k : h * H + 128 * k + 128]


def edges(z, direction, h):
    return jnp.concatenate(
        [
            jnp.concatenate([z.borders[border_at(direction, r, k, h)] for k in range(LT)], 1)
            for r in range(N // 8)
        ],
        0,
    )


class Fold:
    def __init__(self, rising):
        self.rising, self.waiting = rising, {}

    def push(self, value):
        value, step = value[0:8, :] + value[8:16, :], 1
        sub = iota(value.shape, 0)
        while step in self.waiting:
            other = self.waiting.pop(step)
            a, b = (other, value) if self.rising else (value, other)
            low = sub // step % 2 == 0
            value = jnp.where(low, a, b) + pltpu.roll(jnp.where(low, b, a), step, 0)
            step *= 2
        self.waiting[step] = value

    def result(self):
        return self.waiting[8]


def rows_of8(block):
    return pl.ds(pl.multiple_of(block * 8, 8), 8)


def go_forward(z, h):
    lanes = slice(h * H, h * H + H)
    rate2 = jnp.exp(z.dlog[:, lanes]) * (-LOG2E)

    def forward(block, state):
        y = Fold(True)
        for i in range(8):
            t = block * 8 + i
            row = pl.ds(t, 1)
            z.before[t] = state
            d = jnp.exp2(z.deltas[row, lanes] * rate2)
            state = d * state + z.dx[row, lanes] * wide_of(z.bspread[t])
            y.push(state * wide_of(z.cspread[t]))
            z.osum[h, t] = lane_sum(state * z.ocot[row, lanes])
        z.y[rows_of8(block), lanes] = y.result()
        return state

    lax.fori_loop(0, T // 8, forward, edges(z, 0, h))


def go_backward(z, h):
    lanes = slice(h * H, h * H + H)
    rate2 = jnp.exp(z.dlog[:, lanes]) * (-LOG2E)

    def backward(index, carried):
        flow, total = carried
        block = T // 8 - 1 - index
        along, wsum = Fold(False), Fold(False)
        for i in reversed(range(8)):
            t = block * 8 + i
            row = pl.ds(t, 1)
            delta = z.deltas[row, lanes]
            adjoint = z.ocot[row, lanes] * wide_of(z.cspread[t]) + flow
            z.isum[h, t] = lane_sum(adjoint * z.dx[row, lanes])
            along.push(adjoint * wide_of(z.bspread[t]))
            flow = jnp.exp2(delta * rate2) * adjoint
            weighted = flow * z.before[t]
            total = total + weighted * delta
            wsum.push(weighted * rate2)
        z.along[rows_of8(block), lanes] = along.result()
        z.wsum[rows_of8(block), lanes] = wsum.result() * (1.0 / LOG2E)
        return flow, total

    _, total = lax.fori_loop(0, T // 8, backward, (edges(z, 1, h), jnp.zeros((N, H), F32)))
    z.decay_part[:, lanes] = total * (rate2 * (1.0 / LOG2E))


def gather_sums(z):
    unit = jnp.ones((128, 128), BF16)
    place = iota((T * N, 128), 1) - iota((T * N, 128), 0) % N

    def summed(parts):
        return dot_nn((parts[0] + parts[1]).reshape(T * N, 128).astype(BF16), unit)

    both = jnp.where(
        place == 0, summed(z.isum), jnp.where(place == N, summed(z.osum), 0.0)
    ).astype(BF16)
    return dot_nn(z.fold[...], both)


def to_sibling(src, dst, sems):
    me = lax.axis_index(CONTEXT)
    return pltpu.make_async_remote_copy(
        src_ref=src, dst_ref=dst, send_sem=sems.at[0], recv_sem=sems.at[1],
        device_id={CONTEXT: me + 1 - 2 * lax.rem(me, 2)}, device_id_type=MESH,
    )


def send_halves(z, sems, joined, own, other, got, h, pair):
    chip, core = lax.axis_index(CONTEXT) // 2, lax.rem(lax.axis_index(CONTEXT), 2)
    joined, own, other, got = (getattr(z, name) for name in (joined, own, other, got))
    pair.wait()
    joined[h] = (own[h, core].astype(F32) + other[h].astype(F32)).astype(BF16)
    sent = Exchange(joined.at[h], got.at[h], sems.at[h], CHIP)
    sent.start()
    got[h, chip] = joined[h, chip]
    return sent


def layer_kernel(*refs):
    z, given, sem = Refs(), Refs(), Refs()
    refs = list(refs)
    for name, _, _ in INPUTS:
        setattr(given, name, refs.pop(0))
    for name, _, _ in OUTPUTS + INPUTS + SCRATCH:
        setattr(z, name, refs.pop(0))
    for name, _ in SEMS:
        setattr(sem, name, refs.pop(0))
    ctx, ten = lax.axis_index(CONTEXT), lax.axis_index(TENSOR)
    chip, core = ctx // 2, lax.rem(ctx, 2)

    greet(CONTEXT)
    greet(TENSOR)
    loads = {}
    for i, (name, _, _) in enumerate(INPUTS):
        loads[name] = pltpu.make_async_copy(
            getattr(given, name), getattr(z, name), getattr(sem, "in").at[i]
        )

    for name in ("inner", "taps", "shift", "wsel", "gate", "grad", "dlog", "wdelta", "bias", "skip"):
        loads[name].start()

    for name in ("inner", "taps", "shift"):
        loads[name].wait()
    z.pad[16:, :] = z.inner[...].astype(F32)
    convolve(z, 16, T - 16)
    pl.semaphore_wait(pltpu.get_barrier_semaphore(), TEN - 1 + CTX - 1)
    halo = to_neighbour(z.inner.at[pl.ds(T - 16, 16)], z.halo, sem.halo.at[0], sem.halo.at[1], 1)
    halo.start()
    loads["wsel"].wait()
    tail = z.wsel[RANK:PROJ, :]
    z.wtail[0:32, :] = tail
    z.wtail[32:64, :] = jnp.zeros((32, C), BF16)
    z.wtail[64:96, :] = tail
    z.wtail[96:128, :] = jnp.zeros((32, C), BF16)
    project(z, 16, T - 16)
    halo.wait()
    z.pad[0:16, :] = z.halo[...].astype(F32) * (ctx > 0).astype(F32)
    convolve(z, 0, 16)
    project(z, 0, 16)
    scatter = Exchange(z.part, z.got_part, sem.part, TENSOR)
    scatter.start()
    z.got_part[ten] = z.part[ten]

    loads["gate"].wait()
    loads["grad"].wait()
    g = z.gate[...].astype(F32)
    s = sigmoid(g)
    grad = z.grad[...].astype(F32)
    z.ocot[...] = grad * (g * s)
    z.gslope[...] = grad * (s * (1.0 + g * (1.0 - s)))

    scatter.wait_recv()
    total = jnp.sum(z.got_part[...].astype(F32), axis=0)
    bc = total[:, RANK:]
    bc = bc + pltpu.roll(bc, 64, 1)
    z.proj[ten, :, :RANK] = total[:, :RANK].astype(BF16)
    z.proj[ten, :, RANK:] = split_tile(bc)
    gather = Exchange(
        z.proj, z.proj, sem.proj, TENSOR, same=True
    )
    gather.start()
    target = iota((WIDE, WIDE), 0)
    source = iota((WIDE, WIDE), 1)
    place = target % 256
    rest = target - RANK
    order = jnp.where(
        target < RANK,
        (place // 16 * 2 + target // 256) * 17 + place % 16,
        (rest % 16 * 2 + rest // 16) * 17 + 16,
    )
    order = ((order == source) & (target < PROJ)).astype(BF16)
    z.order[...] = order
    loads["wdelta"].wait()
    z.wdperm[...] = dot_nt(z.wdelta[...], order[:, :RANK]).astype(BF16)
    z.wsperm[...] = dot_nn(order[:, :PROJ], z.wsel[...]).astype(BF16)
    z.fold[...] = (iota((T, T * N), 0) == iota((T, T * N), 1) // N).astype(BF16)
    for name in ("dlog", "bias", "skip"):
        loads[name].wait()
    gather.wait_recv()

    flat = z.proj[...].reshape(T, WIDE)
    raw = dot_nt(flat[:, :RANK], z.wdelta[...]) + z.bias[...]
    step = jnp.maximum(raw, 0.0) + jnp.log1p(jnp.exp(-jnp.abs(raw)))
    z.deltas[...] = step
    lengths = jnp.sum(step, axis=0, keepdims=True)
    z.sig[...] = sigmoid(raw)
    z.dx[...] = step * z.conv[...]
    spread(z, flat[:, RANK:])
    ends = Exchange(z.ends, z.got_ends, sem.ends, CONTEXT)
    for h in range(HALVES):
        summarize(z, h, lengths)
        ends.to_core(h, lambda copy: copy.start())

    z.got_ends[ctx] = z.ends[ctx]
    backward = chip // 8
    at_row = pl.ds(pl.multiple_of(lax.rem(chip, 8) // LT * 8, 8), 8)
    at_lane = core * LT + lax.rem(chip, LT)
    rate = jnp.exp(z.dlog[at_row, pl.ds(pl.multiple_of(at_lane * 128, 128), 128)]) * (-LOG2E)
    ends.wait_recv()
    z.decays[...] = jnp.exp2(rate[None] * z.got_ends[:, 8:9, :])
    carried = jnp.zeros((8, 128), F32)
    for i in range(CTX):
        at = i + backward * (CTX - 1 - 2 * i)
        z.back[at] = carried
        carried = z.decays[at] * carried + z.got_ends[at, 0:8, :]
    home = Exchange(z.back, z.borders, sem.back, CONTEXT)
    home.start()
    z.borders[ctx] = z.back[ctx]
    scatter.wait_send()
    gather.wait_send()

    select_part = jnp.zeros((T, WIDE), F32)
    dpairs, deltas, sides = [], [], []
    for h in range(HALVES):
        lanes = slice(h * H, h * H + H)
        home.to_core(h, lambda copy: copy.wait_recv())
        go_forward(z, h)
        if h > 0:
            deltas.append(
                send_halves(z, sem.dsum, "dsum", "dterm", "dpair", "got_d", h - 1, dpairs[h - 1])
            )
        go_backward(z, h)
        near = z.along[:, lanes]
        raw_cot = (z.wsum[:, lanes] + z.conv[:, lanes] * near) * z.sig[:, lanes]
        raw_half = raw_cot.astype(BF16)
        select_part = select_part + dot_nn(raw_half, z.wdperm[lanes, :])
        if h == HALVES - 1:
            select_part = select_part + dot_nt(gather_sums(z).astype(BF16), z.order[:, RANK:])
            z.psel[...] = select_part.astype(BF16).reshape(TEN, ROWS, WIDE)
            scatter2 = Exchange(z.psel, z.got_psel, sem.psel, TENSOR)
            scatter2.start()
            z.got_psel[ten] = z.psel[ten]
        term = dot_tn(flat[:, :RANK], raw_half).astype(BF16).reshape(CHIPS, 2, 16, H)
        z.dterm[h, 0] = term[:, 0]
        z.dterm[h, 1] = term[:, 1]
        dpairs.append(to_sibling(z.dterm.at[h, 1 - core], z.dpair.at[h], sem.dpair.at[h]))
        dpairs[h].start()
        cot, gain, conv = z.ocot[:, lanes], z.skip[:, lanes], z.conv[:, lanes]
        z.gate_grad[:, lanes] = (
            z.gslope[:, lanes] * (z.y[:, lanes] + gain * conv)
        ).astype(BF16)
        z.direct[:, lanes] = gain * cot + z.deltas[:, lanes] * near
        sides.append(
            jnp.concatenate(
                [
                    jnp.sum(raw_cot, axis=0, keepdims=True),
                    jnp.sum(cot * conv, axis=0, keepdims=True),
                ],
                0,
            )
        )

    for k in range(8):
        lanes = slice(128 * k, 128 * k + 128)
        z.early[0, k] = z.decay_part[0:8, lanes]
        z.early[1, k] = z.decay_part[8:16, lanes]
        z.early[:, 8 + k] = jnp.zeros((2, 8, 128), F32)
    epair = to_sibling(z.early.at[1 - core], z.epair, sem.epair)
    epair.start()
    deltas.append(send_halves(z, sem.dsum, "dsum", "dterm", "dpair", "got_d", 1, dpairs[1]))
    epair.wait()
    z.ejoin[...] = z.early[core] + z.epair[...]
    earlies = Exchange(z.ejoin, z.got_early, sem.early, CHIP)
    earlies.start()
    z.got_early[chip] = z.ejoin[chip]
    scatter2.wait_recv()
    z.sel[ten] = jnp.sum(z.got_psel[...].astype(F32), axis=0).astype(BF16)
    gather2 = Exchange(z.sel, z.sel, sem.sel, TENSOR, same=True)
    gather2.start()
    early = jnp.concatenate(sides, 1)
    earlies.wait_recv()
    z.params[core, chip] = jnp.sum(z.got_early[...], axis=0)
    shares = Exchange(z.params.at[core], z.params.at[core], sem.params, CHIP, same=True)
    shares.start()
    gather2.wait_recv()
    select_cot = z.sel[...].reshape(T, WIDE)

    mpairs, mains = [], []
    for h in range(HALVES):
        term = dot_tn(select_cot[:, :RANK], z.half[:, h * H : h * H + H]).astype(BF16)
        z.mterm[h] = term.reshape(2, CHIPS, 16, H)
        mpairs.append(to_sibling(z.mterm.at[h, 1 - core], z.mpair.at[h], sem.mpair.at[h]))
        mpairs[h].start()

    pre_cot = (z.direct[...] + dot_nn(select_cot, z.wsperm[...])) * z.slope[...]
    z.trail[0:T, :] = pre_cot
    z.edge[...] = pre_cot[0:8, :]
    below = to_neighbour(z.edge, z.late, sem.edge.at[0], sem.edge.at[1], -1)
    below.start()
    rows = [early, jnp.sum(pre_cot, axis=0, keepdims=True)]
    for k in range(TAPS):
        rows.append(
            jnp.sum(pre_cot * z.pad[pl.ds(16 - TAPS + 1 + k, T), :], axis=0, keepdims=True)
        )
    rows = jnp.concatenate(rows + [jnp.zeros((1, C), F32)], 0)
    extra = dot_tn(select_cot[:, RANK:], z.half[...])
    for d in range(2):
        mine = jnp.concatenate(
            [rows[:, d * H : d * H + 256], rows[:, d * H + 256 : d * H + 512]], 0
        ).astype(BF16)
        for c in range(CHIPS):
            row = extra[d * CHIPS + c : d * CHIPS + c + 1, :]
            tile = jnp.concatenate(
                [row[:, 128 * k : 128 * k + 128] for k in range(8)] + [jnp.zeros((8, 128), F32)], 0
            )
            z.own[d, c, :, 0:256] = mine
            z.own[d, c, :, 256:384] = tile.astype(BF16)
    opair = to_sibling(z.own.at[1 - core], z.opair, sem.opair)
    opair.start()
    mains.append(send_halves(z, sem.msum, "msum", "mterm", "mpair", "got_m", 0, mpairs[0]))
    opair.wait()
    z.ojoin[...] = (z.own[core].astype(F32) + z.opair[...].astype(F32)).astype(BF16)
    sums = Exchange(z.ojoin, z.got_own, sem.own, CHIP)
    sums.start()
    z.got_own[chip] = z.ojoin[chip]
    mains.append(send_halves(z, sem.msum, "msum", "mterm", "mpair", "got_m", 1, mpairs[1]))

    shares.wait_recv()
    ppair = to_sibling(z.params.at[core], z.params.at[core], sem.ppair)
    ppair.start()
    below.wait()
    z.trail[T:, :] = z.late[...] * (ctx < CTX - 1).astype(F32)
    result = jnp.zeros((T, C), F32)
    for k in range(TAPS):
        result = result + z.taps[k : k + 1, :] * z.trail[pl.ds(TAPS - 1 - k, T), :]
    z.inner_grad[...] = result.astype(BF16)
    for h in range(HALVES):
        deltas[h].wait_recv()
        z.delta_grad[:, h * H : h * H + H] = jnp.sum(z.got_d[h].astype(F32), axis=0)
    ppair.wait()
    for k in range(8):
        lanes = slice(128 * k, 128 * k + 128)
        z.decay_grad[0:8, lanes] = z.params[0, k]
        z.decay_grad[8:16, lanes] = z.params[1, k]
    for exchange in (ends, home, scatter2, gather2, deltas[0], deltas[1], earlies, shares):
        exchange.wait_send()

    sums.wait_recv()
    both = jnp.sum(z.got_own[...].astype(F32), axis=0)
    z.late_sums[core] = jnp.concatenate([both[0:8, 0:256], both[8:16, 0:256]], 1)
    lpair = to_sibling(z.late_sums.at[core], z.late_sums.at[core], sem.lpair)
    lpair.start()
    for k in range(8):
        z.select_grad[16:17, 128 * k : 128 * k + 128] = both[k : k + 1, 256:384]
    for exchange in (sums, mains[0], mains[1]):
        exchange.wait_send()
    for h in range(HALVES):
        mains[h].wait_recv()
        z.select_grad[0:16, h * H : h * H + H] = jnp.sum(z.got_m[h].astype(F32), axis=0)
    lpair.wait()
    for d in range(2):
        lanes = slice(d * H, d * H + H)
        rows = z.late_sums[d]
        z.bias_grad[:, lanes] = rows[0:1, :]
        z.skip_grad[:, lanes] = rows[1:2, :]
        z.shift_grad[:, lanes] = rows[2:3, :]
        z.taps_grad[:, lanes] = rows[3:7, :]


def layer(*args):
    return pl.pallas_call(
        layer_kernel,
        out_shape=[jax.ShapeDtypeStruct(shape, kind) for _, shape, kind in OUTPUTS],
        in_specs=[pl.BlockSpec(memory_space=pl.ANY)] * len(INPUTS),
        out_specs=[VMEM] * len(OUTPUTS),
        scratch_shapes=[pltpu.VMEM(shape, kind) for _, shape, kind in INPUTS + SCRATCH]
        + [pltpu.SemaphoreType.DMA(shape) for _, shape in SEMS],
        compiler_params=pltpu.CompilerParams(
            collective_id=0, has_side_effects=True, vmem_limit_bytes=56 << 20
        ),
        name="layer",
    )(*args)


def finish_kernel(*refs):
    count = len(OUTPUTS)
    for given, out in zip(refs[:count], refs[count:]):
        out[...] = given[...]


def finish(*args):
    return pl.pallas_call(
        finish_kernel,
        out_shape=[jax.ShapeDtypeStruct(shape, kind) for _, shape, kind in OUTPUTS],
        in_specs=[VMEM] * len(OUTPUTS),
        out_specs=[VMEM] * len(OUTPUTS),
        name="finish",
    )(*args)


def body(
    inner_in, gate_in, out_grad, kernel, kernel_shift, select_proj, delta_proj, delta_bias,
    decay_log, skip_gain,
):
    parts = layer(
        inner_in, gate_in, out_grad, kernel.T, kernel_shift[None], select_proj, delta_proj,
        delta_bias[None], decay_log.T, skip_gain[None],
    )
    inner_grad, gate_grad, taps, shift, select, delta, bias, decay, skip = finish(*parts)
    return (
        inner_grad, gate_grad, taps.T, shift[0], select, delta.T, bias[0], decay.T, skip[0],
    )


def solution(mesh):
    return jax.shard_map(
        body,
        mesh=mesh,
        in_specs=(
            P(CONTEXT, TENSOR),
            P(CONTEXT, TENSOR),
            P(CONTEXT, TENSOR),
            P(TENSOR, None),
            P(TENSOR),
            P(None, TENSOR),
            P(TENSOR, None),
            P(TENSOR),
            P(TENSOR, None),
            P(TENSOR),
        ),
        out_specs=(
            P(CONTEXT, TENSOR),
            P(CONTEXT, TENSOR),
            P(TENSOR, None),
            P(TENSOR),
            P(CONTEXT, TENSOR),
            P(TENSOR, CONTEXT),
            P(TENSOR),
            P(TENSOR, None),
            P(TENSOR),
        ),
        check_vma=False,
    )
```
